512 devices in a mesh: seq: 64 (over x, z_lo, core), head: 8 (over y, z_hi).
Axes of the slice: x: 4, y: 4, z: 16 (z_hi: 2, z_lo: 8; z = z_hi * 8 + z_lo), core: 2. Of those that a mesh axis runs over, the one named last changes fastest.
Arguments:
- q_lat: bfloat16 [8192, 64, 512], P('seq', 'head'), may hold values from -6 to 6
- q_rope: bfloat16 [8192, 4096], P('seq', 'head'), may hold values from -6 to 6
- d_out: bfloat16 [8192, 64, 512], P('seq', 'head'), may hold values from -12 to 12
- latent: bfloat16 [8192, 512], P('seq'), may hold values from -6 to 6
- key_rope: bfloat16 [64, 8192], P(None, 'seq'), may hold values from -6 to 6
- forward_dot: float32 [64, 8192], P('head', 'seq'), may hold values from -120 to 120
- log_total: float32 [64, 8192], P('head', 'seq'), may hold values from 6 to 9
- block_order: int32 [128], replicated, may hold values from 0 to 127, as said below
Outputs:
- grad_q_lat: bfloat16 [8192, 64, 512], P('seq', 'head')
- grad_q_rope: bfloat16 [8192, 4096], P('seq', 'head')
- grad_latent: bfloat16 [8192, 512], P(('seq', 'head'))
- grad_key_rope: bfloat16 [8192, 64], P(('seq', 'head'))
The draws below stay inside these ranges and needn't reach their ends.
Inputs may be any that keep to these rules, and one draw needn't show every extreme that they name: `block_order`: each seq index's two entries are a and 127 - a in either order, and over the 64 indices the values a run through 0 to 63 once each.
All inputs are finite; a program needn't handle non-finite values.
Results may differ from the reference program's by a relative error of at most 0.008.
Values may be sent and summed in bfloat16 or wider, within the bound.
No kernel may reach another device: no remote copies, remote signals or barrier semaphores. Data moves between devices by JAX's collectives and lax.ppermute only.
A program may use at most 64 MiB of HBM per device.

```python
import jax
import jax.numpy as jnp
from jax import lax

LAT = 512
ROPE = 64
SPAN = 4
TOK_DEV = 128
CYCLE = 64
BLK = 64
SLOTS = 128
TOKENS = 8192
HEADS = 64


def draw_block_order(key, part):
    key = jax.random.fold_in(key, 5)
    lower_ids = jax.random.permutation(jax.random.fold_in(key, 1), CYCLE).astype(jnp.int32)
    flipped = jax.random.randint(jax.random.fold_in(key, 2), (CYCLE,), 0, 2)
    leading = jnp.where(flipped == 1, 2 * CYCLE - 1 - lower_ids, lower_ids)
    trailing = 2 * CYCLE - 1 - leading
    return jnp.stack([leading, trailing], axis=-1).reshape(SLOTS).astype(jnp.int32)


def level_of(stream_key, shape, split, smallest, top_value):
    factor_of, own = 1.0, jax.random.fold_in(stream_key, 6)
    for dim, blocks in split:
        heights = jnp.exp(jax.random.uniform(jax.random.fold_in(own, dim), (blocks,), jnp.float32, smallest / len(split), top_value / len(split)))
        factor_of = factor_of * jnp.repeat(heights, shape[dim] // blocks).reshape([-1 if axis == dim else 1 for axis in range(len(shape))])
    return factor_of


def scatter_about(key, dims, deviation, reach, pieces=(), kind=jnp.bfloat16):
    factor_of = level_of(key, dims, pieces, -0.22, 0.18) if pieces else 1.0
    values = jax.random.normal(key, dims, jnp.float32) * deviation * factor_of
    return jnp.minimum(jnp.maximum(values, -reach), reach).astype(kind)


def setup_inputs(seed: int = 0) -> dict:
    key_of = jax.random.split(jax.random.key(seed), 9)
    q_lat = scatter_about(key_of[0], (TOKENS, HEADS, LAT), 1.0, 6.0, ((0, 64), (1, 8)))
    q_rope = scatter_about(key_of[1], (TOKENS, HEADS * ROPE), 1.0, 6.0, ((0, 64), (1, 8)))
    d_out = scatter_about(key_of[2], (TOKENS, HEADS, LAT), 2.0, 12.0, ((0, 64), (1, 8)))
    latent = scatter_about(key_of[3], (TOKENS, LAT), 1.0, 6.0, ((0, 64),))
    key_rope = scatter_about(key_of[4], (ROPE, TOKENS), 1.0, 6.0, ((1, 64),))
    forward_dot = scatter_about(key_of[5], (HEADS, TOKENS), 20.0, 120.0, ((0, 8), (1, 64)), jnp.float32)
    log_total = jnp.clip(6.0 + 3.0 * jax.random.uniform(key_of[6], (HEADS, TOKENS), jnp.float32) ** level_of(key_of[6], (HEADS, TOKENS), ((0, 8), (1, 64)), -0.2, 0.2), 6.0, 9.0)
    block_order = draw_block_order(jax.random.fold_in(key_of[8], 71), 0)
    return {"q_lat": q_lat, "q_rope": q_rope, "d_out": d_out, "latent": latent, "key_rope": key_rope, "forward_dot": forward_dot, "log_total": log_total, "block_order": block_order}


SOFTMAX_SCALE = 192.0 ** -0.5
MASKED = -1.0e30


def mult(form, left, right):
    return jnp.einsum(form, left, right, precision=lax.Precision.HIGHEST)


def reference(q_lat, q_rope, d_out, latent, key_rope, forward_dot, log_total, block_order):
    window = SPAN * TOK_DEV
    token_ids = jnp.arange(TOK_DEV, dtype=jnp.int32)
    block_pairs = block_order.reshape(CYCLE, 2).astype(jnp.int32)
    positions = (jnp.where(token_ids[None, :] < BLK, block_pairs[:, 0:1], block_pairs[:, 1:2]) * BLK
                 + token_ids[None, :] % BLK).astype(jnp.int32)
    shard_ids = jnp.arange(CYCLE, dtype=jnp.int32)
    step_ids = jnp.arange(SPAN, dtype=jnp.int32)
    sources = ((shard_ids[:, None] - step_ids[None, :]) % CYCLE).astype(jnp.int32)
    key_shards = latent.astype(jnp.float32).reshape(CYCLE, TOK_DEV, LAT)
    rope_shards = key_rope.astype(jnp.float32).T.reshape(CYCLE, TOK_DEV, ROPE)
    key_window = key_shards[sources].reshape(CYCLE, window, LAT)
    rope_window = rope_shards[sources].reshape(CYCLE, window, ROPE)
    key_positions = positions[sources].reshape(CYCLE, window)
    visible = key_positions[:, None, :] <= positions[:, :, None]

    queries = q_lat.reshape(CYCLE, TOK_DEV, HEADS, LAT).transpose(2, 0, 1, 3)
    rope_queries = q_rope.reshape(CYCLE, TOK_DEV, HEADS, ROPE).transpose(2, 0, 1, 3)
    out_grads = d_out.reshape(CYCLE, TOK_DEV, HEADS, LAT).transpose(2, 0, 1, 3)
    head_totals = log_total.reshape(HEADS, CYCLE, TOK_DEV)
    head_dots = forward_dot.reshape(HEADS, CYCLE, TOK_DEV)

    def one_head(totals, inputs):
        q_head, rope_head, grad_head, total_head, dot_head = inputs
        q_head = q_head.astype(jnp.float32)
        rope_head = rope_head.astype(jnp.float32)
        grad_head = grad_head.astype(jnp.float32)
        scores = SOFTMAX_SCALE * (mult("rtd,rwd->rtw", q_head, key_window)
                                  + mult("rte,rwe->rtw", rope_head, rope_window))
        shifted = jnp.where(visible, scores - total_head[:, :, None], MASKED)
        probs = jnp.exp(shifted)
        dprobs = mult("rtd,rwd->rtw", grad_head, key_window)
        dscores = (SOFTMAX_SCALE * probs * (dprobs - dot_head[:, :, None])).astype(jnp.bfloat16)
        probs_low = probs.astype(jnp.bfloat16)
        dscores_wide = dscores.astype(jnp.float32)
        probs_wide = probs_low.astype(jnp.float32)
        grad_query = mult("rtw,rwd->rtd", dscores_wide, key_window).astype(jnp.bfloat16)
        grad_rope = mult("rtw,rwe->rte", dscores_wide, rope_window).astype(jnp.bfloat16)
        latent_total = (totals[0] + mult("rtw,rtd->rwd", dscores_wide, q_head)
                        + mult("rtw,rtd->rwd", probs_wide, grad_head))
        keyrope_total = totals[1] + mult("rtw,rte->rwe", dscores_wide, rope_head)
        return (latent_total, keyrope_total), (grad_query, grad_rope)

    zero_totals = (jnp.zeros((CYCLE, window, LAT), jnp.float32), jnp.zeros((CYCLE, window, ROPE), jnp.float32))
    (latent_total, keyrope_total), (grad_query, grad_rope) = lax.scan(
        one_head, zero_totals, (queries, rope_queries, out_grads, head_totals, head_dots))
    grad_q_lat = grad_query.transpose(1, 2, 0, 3).reshape(TOKENS, HEADS, LAT)
    grad_q_rope = grad_rope.transpose(1, 2, 0, 3).reshape(TOKENS, HEADS * ROPE)
    latent_steps = latent_total.reshape(CYCLE, SPAN, TOK_DEV, LAT)
    keyrope_steps = keyrope_total.reshape(CYCLE, SPAN, TOK_DEV, ROPE)
    latent_home = jnp.zeros((CYCLE, TOK_DEV, LAT), jnp.float32)
    keyrope_home = jnp.zeros((CYCLE, TOK_DEV, ROPE), jnp.float32)
    for step_idx in range(SPAN):
        latent_home = latent_home + jnp.roll(latent_steps[:, step_idx], -step_idx, axis=0)
        keyrope_home = keyrope_home + jnp.roll(keyrope_steps[:, step_idx], -step_idx, axis=0)
    grad_latent = latent_home.reshape(TOKENS, LAT).astype(jnp.bfloat16)
    grad_key_rope = keyrope_home.reshape(TOKENS, ROPE).astype(jnp.bfloat16)
    return (grad_q_lat, grad_q_rope, grad_latent, grad_key_rope)
```

```python
import jax
import jax.numpy as jnp
from jax import lax
from jax.experimental import pallas as pl
from jax.experimental.pallas import tpu as pltpu
from jax.sharding import PartitionSpec as P

SPAN = 4
SOFTMAX_SCALE = 192.0 ** (-0.5)
BLK = 64
RUN = 16
ORDER = (0, 2, 1, 3)


def shift(value, by):
    seqs, heads = lax.axis_size("seq"), lax.axis_size("head")
    pairs = []
    for i in range(seqs):
        j = (i + by) % seqs
        for h in range(heads):
            pairs.append((i * heads + h, j * heads + (h ^ 1 if i // RUN != j // RUN else h)))
    return lax.ppermute(value, ("seq", "head"), pairs)


def nt(a, b):
    return lax.dot_general(a, b, (((1,), (1,)), ((), ())), preferred_element_type=jnp.float32)


def nn(a, b):
    return lax.dot_general(a, b, (((1,), (0,)), ((), ())), preferred_element_type=jnp.float32)


def tn(a, b):
    return lax.dot_general(a, b, (((0,), (0,)), ((), ())), preferred_element_type=jnp.float32)


def rope_of(packed):
    wide = jnp.concatenate([packed[:, 128 * b : 128 * (b + 1)] for b in range(4)], axis=0)
    return wide.astype(jnp.float32).T.astype(jnp.bfloat16)


def attention_kernel(
    index_ref, order_ref, own_ref, ka_ref, kb_ref, kc_ref, q_ref, qr_ref, do_ref, dot_ref, tot_ref,
    gq_ref, gqr_ref, send_ref, keep_ref,
    rope_ref,
):
    me = index_ref[0]
    seqs = order_ref.shape[0] // 2
    shard_refs = {0: own_ref, 2: ka_ref, 1: kb_ref, 3: kc_ref}
    rows = q_ref.shape[0] // 2
    heads = rows // BLK
    own_first, own_second = order_ref[2 * me], order_ref[2 * me + 1]
    high = jnp.where(own_first > own_second, 0, 1)
    low_mine = jnp.minimum(own_first, own_second)
    high_mine = jnp.maximum(own_first, own_second)
    upper = pl.ds(pl.multiple_of(high * rows, rows), rows)
    lower = pl.ds(pl.multiple_of((1 - high) * rows, rows), rows)

    low_keys, high_keys, low_ropes, high_ropes = [], [], [], []
    low_blocks, high_blocks, low_at, high_at = [], [], [], []
    for place, s in enumerate(ORDER):
        ref = shard_refs[s]
        other = lax.rem(me + seqs - s, seqs)
        first, second = order_ref[2 * other], order_ref[2 * other + 1]
        low_slot = jnp.where(first < second, 0, 1)
        at_low = pl.multiple_of(low_slot * BLK, BLK)
        at_high = pl.multiple_of((1 - low_slot) * BLK, BLK)
        rope_ref[place] = rope_of(ref[2 * BLK :, :])
        low_keys.append(ref[pl.ds(at_low, BLK), :])
        high_keys.append(ref[pl.ds(at_high, BLK), :])
        low_ropes.append(rope_ref[place, pl.ds(at_low, BLK), :])
        high_ropes.append(rope_ref[place, pl.ds(at_high, BLK), :])
        low_blocks.append(jnp.minimum(first, second))
        high_blocks.append(jnp.maximum(first, second))
        low_at.append(at_low)
        high_at.append(at_high)
    low_keys = jnp.concatenate(low_keys, axis=0)
    high_keys = jnp.concatenate(high_keys, axis=0)
    low_ropes = jnp.concatenate(low_ropes, axis=0)
    high_ropes = jnp.concatenate(high_ropes, axis=0)

    ahead = (
        lax.broadcasted_iota(jnp.int32, (BLK, rows), 1) // heads
        - lax.broadcasted_iota(jnp.int32, (BLK, rows), 0)
    )

    def block(part, row_block, keys, ropes, key_blocks):
        q, qr, do = q_ref[part, :], qr_ref[part, :], do_ref[part, :]
        total, dots = tot_ref[:, part], dot_ref[:, part]
        scores = SOFTMAX_SCALE * (nt(keys, q) + nt(ropes, qr))
        probs = jnp.exp(scores - total)
        if key_blocks is not None:
            seen = jnp.concatenate(
                [ahead >= (b - row_block) * BLK for b in key_blocks], axis=0
            )
            probs = jnp.where(seen, probs, 0.0)
        dprobs = nt(keys, do)
        dscores = (SOFTMAX_SCALE * probs * (dprobs - dots)).astype(jnp.bfloat16)
        probs_low = probs.astype(jnp.bfloat16)
        return (
            tn(dscores, keys),
            tn(dscores, ropes),
            nn(dscores, q) + nn(probs_low, do),
            nn(dscores, qr),
        )

    gq_a, gqr_a, lat_a, rope_a = block(upper, high_mine, low_keys, low_ropes, None)
    gq_b, gqr_b, lat_b, rope_b = block(upper, high_mine, high_keys, high_ropes, high_blocks)
    gq_c, gqr_c, lat_c, rope_c = block(lower, low_mine, low_keys, low_ropes, low_blocks)
    gq_ref[upper, :] = (gq_a + gq_b).astype(jnp.bfloat16)
    gqr_ref[upper, :] = (gqr_a + gqr_b).astype(jnp.bfloat16)
    gq_ref[lower, :] = gq_c.astype(jnp.bfloat16)
    gqr_ref[lower, :] = gqr_c.astype(jnp.bfloat16)
    low_lat, low_rope = lat_a + lat_c, rope_a + rope_c
    blank = jnp.zeros((BLK, 64), jnp.float32)
    for place in range(SPAN):
        out_ref, base = (keep_ref, place) if place < 2 else (send_ref, place - 2)
        cut = slice(place * BLK, (place + 1) * BLK)
        for at, lat, rope in ((low_at, low_lat, low_rope), (high_at, lat_b, rope_b)):
            value = jnp.concatenate([lat[cut], rope[cut], blank], axis=1)
            out_ref[pl.ds(base * 2 * BLK + at[place], BLK), :] = value.astype(out_ref.dtype)


def attention(index, order, own, ka, kb, kc, q, qr, do, dots, totals):
    rows, width = q.shape
    vmem = pl.BlockSpec(memory_space=pltpu.VMEM)
    smem = pl.BlockSpec(memory_space=pltpu.SMEM)
    return pl.pallas_call(
        attention_kernel,
        out_shape=(
            jax.ShapeDtypeStruct((rows, width), jnp.bfloat16),
            jax.ShapeDtypeStruct((rows, 64), jnp.bfloat16),
            jax.ShapeDtypeStruct((256, 640), jnp.bfloat16),
            jax.ShapeDtypeStruct((256, 640), jnp.float32),
        ),
        in_specs=[smem, smem] + [vmem] * 9,
        out_specs=[vmem] * 4,
        scratch_shapes=[pltpu.VMEM((SPAN, 128, 64), jnp.bfloat16)],
        compiler_params=pltpu.CompilerParams(vmem_limit_bytes=48 * 2**20),
        cost_estimate=pl.CostEstimate(
            flops=3_000_000_000, bytes_accessed=5_000_000, transcendentals=400_000
        ),
    )(index, order, own, ka, kb, kc, q, qr, do, dots, totals)


def shards(q_lat, q_rope, d_out, latent, key_rope, forward_dot, log_total, block_order):
    tokens, heads, width = q_lat.shape
    rows = tokens * heads
    own = jnp.concatenate(
        [latent, jnp.concatenate([key_rope[16 * b : 16 * (b + 1)] for b in range(4)], axis=1)], axis=0
    )
    two_back = shift(own, 2)
    one_back = shift(own, 1)
    three_back = shift(two_back, 1)
    index = lax.axis_index("seq").astype(jnp.int32).reshape(1)
    grad_q, grad_qr, send, keep = attention(
        index,
        block_order,
        own,
        two_back,
        one_back,
        three_back,
        q_lat.reshape(rows, width),
        q_rope.reshape(rows, 64),
        d_out.reshape(rows, width),
        forward_dot.T.reshape(1, rows),
        log_total.T.reshape(1, rows),
    )
    near = shift(send, -1)
    far = shift((keep[128:] + near[128:].astype(jnp.float32)).astype(jnp.bfloat16), -2)
    mine = keep[:128] + near[:128].astype(jnp.float32) + far.astype(jnp.float32)
    parts = lax.all_to_all(mine.astype(jnp.bfloat16), "head", 0, 0, tiled=True)
    whole = parts.reshape(lax.axis_size("head"), -1, 640).astype(jnp.float32).sum(0)
    return (
        grad_q.reshape(tokens, heads, width),
        grad_qr.reshape(tokens, heads * 64),
        whole[:, :512].astype(jnp.bfloat16),
        whole[:, 512:576].astype(jnp.bfloat16),
    )


def solution(mesh):
    return jax.shard_map(
        shards,
        mesh=mesh,
        in_specs=(
            P("seq", "head", None),
            P("seq", "head"),
            P("seq", "head", None),
            P("seq", None),
            P(None, "seq"),
            P("head", "seq"),
            P("head", "seq"),
            P(),
        ),
        out_specs=(
            P("seq", "head", None),
            P("seq", "head"),
            P(("seq", "head"), None),
            P(("seq", "head"), None),
        ),
        check_vma=False,
    )
```

```python
import jax
import jax.numpy as jnp
from jax import lax
from jax.experimental import pallas as pl
from jax.experimental.pallas import tpu as pltpu
from jax.sharding import PartitionSpec as P

SPAN = 4
SOFTMAX_SCALE = 192.0 ** (-0.5)
BLK = 64
RUN = 16
ORDER = (0, 2, 1, 3)


def permute(value, to):
    seqs, heads = lax.axis_size("seq"), lax.axis_size("head")
    pairs = []
    for i in range(seqs):
        if to(i) is None:
            continue
        j = to(i) % seqs
        for h in range(heads):
            pairs.append((i * heads + h, j * heads + (h ^ 1 if i // RUN != j // RUN else h)))
    return lax.ppermute(value, ("seq", "head"), pairs)


def shift(value, by):
    return permute(value, lambda i: i + by)


def swap_cores(value):
    return permute(value, lambda i: i ^ 1)


def nt(a, b):
    return lax.dot_general(a, b, (((1,), (1,)), ((), ())), preferred_element_type=jnp.float32)


def nn(a, b):
    return lax.dot_general(a, b, (((1,), (0,)), ((), ())), preferred_element_type=jnp.float32)


def tn(a, b):
    return lax.dot_general(a, b, (((0,), (0,)), ((), ())), preferred_element_type=jnp.float32)


def rope_of(packed):
    wide = jnp.concatenate([packed[:, 128 * b : 128 * (b + 1)] for b in range(4)], axis=0)
    return wide.astype(jnp.float32).T.astype(jnp.bfloat16)


def gather_keys(order_ref, me, shards_in_order, refs, bases, rope_ref):
    seqs = order_ref.shape[0] // 2
    low, high = [], []
    for place, s in enumerate(shards_in_order):
        other = lax.rem(me + seqs - s, seqs)
        first, second = order_ref[2 * other], order_ref[2 * other + 1]
        low_slot = jnp.where(first < second, 0, 1)
        at_low = pl.multiple_of(low_slot * BLK, BLK)
        at_high = pl.multiple_of((1 - low_slot) * BLK, BLK)
        rope_ref[place] = rope_of(refs[place][pl.ds(bases[place] + 2 * BLK, 16), :])
        for out, at, pos in ((low, at_low, jnp.minimum(first, second)), (high, at_high, jnp.maximum(first, second))):
            out.append((refs[place][pl.ds(pl.multiple_of(bases[place] + at, 16), BLK), :], rope_ref[place, pl.ds(at, BLK), :], pos, at))
    both = low + high
    keys = jnp.concatenate([x[0] for x in both], axis=0)
    ropes = jnp.concatenate([x[1] for x in both], axis=0)
    return keys, ropes, [x[2] for x in both], [x[3] for x in both]


def own_place(order_ref, me, rows):
    first, second = order_ref[2 * me], order_ref[2 * me + 1]
    high = jnp.where(first > second, 0, 1)
    upper = pl.multiple_of(high * rows, rows)
    lower = pl.multiple_of((1 - high) * rows, rows)
    return jnp.minimum(first, second), jnp.maximum(first, second), lower, upper


def tile(keys, ropes, key_blocks, row_block, q, qr, do, total, dots):
    rows = q.shape[0]
    scores = SOFTMAX_SCALE * (nt(keys, q) + nt(ropes, qr))
    probs = jnp.exp(scores - total)
    ahead = (
        lax.broadcasted_iota(jnp.int32, (BLK, rows), 1) // (rows // BLK)
        - lax.broadcasted_iota(jnp.int32, (BLK, rows), 0)
    )
    pieces = []
    for n, key_block in enumerate(key_blocks):
        piece = probs[n * BLK : (n + 1) * BLK]
        if key_block is not None:
            piece = jnp.where(ahead >= (key_block - row_block) * BLK, piece, 0.0)
        pieces.append(piece)
    probs = jnp.concatenate(pieces, axis=0)
    dprobs = nt(keys, do)
    dscores = (SOFTMAX_SCALE * probs * (dprobs - dots)).astype(jnp.bfloat16)
    return probs.astype(jnp.bfloat16), dscores


def pack_kernel(lat_hbm, rope_hbm, own_ref, sems):
    copies = [pltpu.make_async_copy(lat_hbm, own_ref.at[pl.ds(0, 128), :], sems.at[4])]
    for b in range(4):
        copies.append(
            pltpu.make_async_copy(
                rope_hbm.at[pl.ds(16 * b, 16), :],
                own_ref.at[pl.ds(128, 16), pl.ds(128 * b, 128)],
                sems.at[b],
            )
        )
    for copy in copies:
        copy.start()
    for copy in copies:
        copy.wait()


def spread(values):
    heads, tokens = values.shape
    rows = heads * tokens
    pieces, rest = [], values
    for _ in range(3):
        piece = rest.astype(jnp.bfloat16)
        rest = rest - piece.astype(jnp.float32)
        pieces.append(piece)
    column = lax.broadcasted_iota(jnp.int32, (tokens, rows), 1)
    token = lax.broadcasted_iota(jnp.int32, (tokens, rows), 0)
    pick = jnp.where(column // heads == token, 1.0, 0.0).astype(jnp.bfloat16)
    wide = (nn(pieces[0], pick) + nn(pieces[1], pick)) + nn(pieces[2], pick)
    column = lax.broadcasted_iota(jnp.int32, (heads, rows), 1)
    head = lax.broadcasted_iota(jnp.int32, (heads, rows), 0)
    return jnp.sum(jnp.where(lax.rem(column, heads) == head, wide, 0.0), axis=0, keepdims=True)


def prep_kernel(q_hbm, do_hbm, dot_ref, tot_ref, q_ref, do_ref, dots_ref, tots_ref, sems):
    copies = []
    rows = q_ref.shape[0] // 4
    for n in range(4):
        for m, (hbm, ref) in enumerate(((q_hbm, q_ref), (do_hbm, do_ref))):
            part = pl.ds(n * rows, rows)
            copies.append(pltpu.make_async_copy(hbm.at[part, :], ref.at[part, :], sems.at[n, m]))
    for copy in copies:
        copy.start()
    dots_ref[...] = spread(dot_ref[...])
    tots_ref[...] = spread(tot_ref[...])
    for copy in copies:
        copy.wait()


def early_kernel(
    order_ref, own_ref, ka_ref, q_ref, qr_ref, do_ref, dot_ref, tot_ref,
    ds_ref, lat_ref, grope_ref, keys_ref, ropes_ref,
    rope_ref,
):
    me = lax.axis_index("seq")
    rows = q_ref.shape[0] // 2
    _, high_mine, _, upper = own_place(order_ref, me, rows)
    part = pl.ds(upper, rows)
    keys, ropes, blocks, _ = gather_keys(order_ref, me, ORDER[:2], (own_ref, ka_ref), (0, 0), rope_ref)
    keys_ref[...] = keys
    ropes_ref[...] = ropes
    q, qr, do = q_ref[part, :], qr_ref[part, :], do_ref[part, :]
    probs, ds = tile(
        keys, ropes, [None, None] + blocks[2:], high_mine, q, qr, do, tot_ref[:, part], dot_ref[:, part]
    )
    ds_ref[...] = ds
    lat_ref[...] = nn(ds, q) + nn(probs, do)
    grope_ref[...] = nn(ds, qr)


def main_kernel(
    order_ref, pair_ref, three_ref, q_ref, qr_ref, do_ref, dot_ref, tot_ref, lat_ref, grope_ref, keys_a_ref, ropes_a_ref,
    sib_ref, far_ref, keep_ref, ds_b_ref, ds_c_ref, keys_b_ref, ropes_b_ref,
    rope_ref,
):
    me = lax.axis_index("seq")
    even = lax.rem(me, 2) == 0
    rows = q_ref.shape[0] // 2
    low_mine, high_mine, lower, upper = own_place(order_ref, me, rows)
    seqs = order_ref.shape[0] // 2
    keys, ropes, blocks, at_b = gather_keys(
        order_ref, me, ORDER[2:], (pair_ref, three_ref), (0, 0), rope_ref
    )
    keys_b_ref[...] = keys
    ropes_b_ref[...] = ropes
    low_blocks, at_a = [], []
    for s in ORDER[:2]:
        other = lax.rem(me + seqs - s, seqs)
        first, second = order_ref[2 * other], order_ref[2 * other + 1]
        low_blocks.append(jnp.minimum(first, second))
        at_a.append(pl.multiple_of(jnp.where(first < second, 0, BLK), BLK))
    at_a += [pl.multiple_of(BLK - at, BLK) for at in at_a]
    low_keys = jnp.concatenate([keys_a_ref[: 2 * BLK], keys[: 2 * BLK]], axis=0)
    low_ropes = jnp.concatenate([ropes_a_ref[: 2 * BLK], ropes[: 2 * BLK]], axis=0)

    part = pl.ds(upper, rows)
    q, qr, do = q_ref[part, :], qr_ref[part, :], do_ref[part, :]
    probs, ds = tile(
        keys, ropes, [None, None] + blocks[2:], high_mine, q, qr, do, tot_ref[:, part], dot_ref[:, part]
    )
    ds_b_ref[...] = ds
    lat_b = nn(ds, q) + nn(probs, do)
    grope_b = nn(ds, qr)

    part = pl.ds(lower, rows)
    q, qr, do = q_ref[part, :], qr_ref[part, :], do_ref[part, :]
    probs, ds = tile(
        low_keys, low_ropes, low_blocks + blocks[:2], low_mine, q, qr, do, tot_ref[:, part], dot_ref[:, part]
    )
    ds_c_ref[...] = ds
    lat_c = nn(ds, q) + nn(probs, do)
    grope_c = nn(ds, qr)

    half = 2 * BLK
    blank = jnp.zeros((BLK, 64), jnp.float32)

    def whole(lat, grope, more, n):
        cut = slice(n * BLK, (n + 1) * BLK)
        lat_n, grope_n = lat[cut], grope[cut]
        if n < 2:
            add = slice(more + n * BLK, more + (n + 1) * BLK)
            lat_n, grope_n = lat_n + lat_c[add], grope_n + grope_c[add]
        return jnp.concatenate([lat_n, grope_n, blank], axis=1)

    lat_a, grope_a = lat_ref[...], grope_ref[...]
    for n, at in enumerate(at_a):
        keep_ref[pl.ds((n % 2) * half + at, BLK), :] = whole(lat_a, grope_a, 0, n)
    for n in (0, 2):
        one = whole(lat_b, grope_b, half, n)
        three = whole(lat_b, grope_b, half, n + 1)
        far_ref[pl.ds(at_b[n + 1], BLK), :] = three.astype(jnp.bfloat16)
        sib_ref[pl.ds(at_b[n], BLK), :] = jnp.where(even, 0.0, one).astype(jnp.bfloat16)
        second = half + jnp.where(even, at_b[n], at_b[n + 1])
        sib_ref[pl.ds(pl.multiple_of(second, BLK), BLK), :] = jnp.where(even, one, three).astype(jnp.bfloat16)


def query_kernel(
    order_ref, ds_a_ref, ds_b_ref, ds_c_ref, keys_a_ref, ropes_a_ref, keys_b_ref, ropes_b_ref, gq_ref, gqr_ref
):
    me = lax.axis_index("seq")
    rows = ds_a_ref.shape[1]
    _, _, lower, upper = own_place(order_ref, me, rows)
    half = 2 * BLK
    low_keys = jnp.concatenate([keys_a_ref[:half], keys_b_ref[:half]], axis=0)
    low_ropes = jnp.concatenate([ropes_a_ref[:half], ropes_b_ref[:half]], axis=0)
    ds_a, ds_b, ds_c = ds_a_ref[...], ds_b_ref[...], ds_c_ref[...]
    part = pl.ds(upper, rows)
    gq_ref[part, :] = (tn(ds_a, keys_a_ref[...]) + tn(ds_b, keys_b_ref[...])).astype(jnp.bfloat16)
    gqr_ref[part, :] = (tn(ds_a, ropes_a_ref[...]) + tn(ds_b, ropes_b_ref[...])).astype(jnp.bfloat16)
    part = pl.ds(lower, rows)
    gq_ref[part, :] = tn(ds_c, low_keys).astype(jnp.bfloat16)
    gqr_ref[part, :] = tn(ds_c, low_ropes).astype(jnp.bfloat16)


VMEM = pl.BlockSpec(memory_space=pltpu.VMEM)
SMEM = pl.BlockSpec(memory_space=pltpu.SMEM)
HBM = pl.BlockSpec(memory_space=pltpu.HBM)


def in_hbm(value):
    return pltpu.with_memory_space_constraint(value, pltpu.HBM)


def call(kernel, args, in_specs, outs, scratch, gflop, aliases={}):
    return pl.pallas_call(
        kernel,
        out_shape=tuple(jax.ShapeDtypeStruct(shape, dtype) for shape, dtype in outs),
        in_specs=in_specs,
        out_specs=(VMEM,) * len(outs),
        scratch_shapes=scratch,
        input_output_aliases=aliases,
        compiler_params=pltpu.CompilerParams(vmem_limit_bytes=32 * 2**20),
        cost_estimate=pl.CostEstimate(
            flops=int(gflop * 1e9), bytes_accessed=int(gflop * 2e6), transcendentals=int(gflop * 1e5)
        ),
    )(*args)


def share_kernel(parts_ref, keep_ref, send_ref):
    whole = parts_ref[0].astype(jnp.float32)
    for n in range(1, parts_ref.shape[0]):
        whole = whole + parts_ref[n].astype(jnp.float32)
    rows = keep_ref.shape[0]
    first = lax.rem(lax.axis_index("head"), 2) == 0
    keep_ref[...] = jnp.where(first, whole[:rows], whole[rows:])
    send_ref[...] = jnp.where(first, whole[rows:], whole[:rows]).astype(jnp.bfloat16)


def last_kernel(keep_ref, got_ref, lat_ref, rope_ref):
    whole = keep_ref[...] + got_ref[...].astype(jnp.float32)
    lat_ref[...] = whole[:, :512].astype(jnp.bfloat16)
    rope_ref[...] = whole[:, 512:576].astype(jnp.bfloat16)


def shards(q_lat, q_rope, d_out, latent, key_rope, forward_dot, log_total, block_order):
    tokens, heads, width = q_lat.shape
    rows = tokens * heads
    half, bf16, f32 = rows // 2, jnp.bfloat16, jnp.float32
    (own,) = call(
        pack_kernel,
        (in_hbm(latent), in_hbm(key_rope)),
        [HBM] * 2,
        [((tokens + 16, width), bf16)],
        [pltpu.SemaphoreType.DMA((5,))],
        0.0,
    )
    two_back = shift(own, 2)
    q, do, dots, sums = call(
        prep_kernel,
        (in_hbm(q_lat.reshape(rows, width)), in_hbm(d_out.reshape(rows, width)), forward_dot, log_total),
        [HBM, HBM, VMEM, VMEM],
        [((rows, width), bf16), ((rows, width), bf16), ((1, rows), f32), ((1, rows), f32)],
        [pltpu.SemaphoreType.DMA((4, 2))],
        0.0,
    )
    qr = q_rope.reshape(rows, 64)
    two_back, q, do, dots, sums, qr = lax.optimization_barrier((two_back, q, do, dots, sums, qr))
    three_back = shift(two_back, 1)
    pair = shift(own, 1)
    ds_a, lat_a, grope_a, keys_a, ropes_a = call(
        early_kernel,
        (block_order, own, two_back, q, qr, do, dots, sums),
        [SMEM] + [VMEM] * 7,
        [((256, half), bf16), ((256, width), f32), ((256, 64), f32), ((256, width), bf16), ((256, 64), bf16)],
        [pltpu.VMEM((2, 128, 64), bf16)],
        0.0,
    )
    sib, far, keep, ds_b, ds_c, keys_b, ropes_b = call(
        main_kernel,
        (block_order, pair, three_back, q, qr, do, dots, sums, lat_a, grope_a, keys_a, ropes_a),
        [SMEM] + [VMEM] * 11,
        [
            ((256, 640), bf16),
            ((128, 640), bf16),
            ((256, 640), f32),
            ((256, half), bf16),
            ((256, half), bf16),
            ((256, width), bf16),
            ((256, 64), bf16),
        ],
        [pltpu.VMEM((2, 128, 64), bf16)],
        1.6,
    )
    near = swap_cores(sib)
    from_three = permute(far, lambda i: None if i % 2 else i - 3)
    grad_q, grad_qr = call(
        query_kernel,
        (block_order, ds_a, ds_b, ds_c, keys_a, ropes_a, keys_b, ropes_b),
        [SMEM] + [VMEM] * 7,
        [((rows, width), bf16), ((rows, 64), bf16)],
        [],
        0.8,
    )
    grad_qr = grad_qr.reshape(tokens, heads * 64)
    near = near.astype(f32)
    from_two = shift((keep[128:] + near[128:]).astype(bf16), -2)
    mine = (keep[:128] + near[:128] + from_three.astype(f32) + from_two.astype(f32)).astype(bf16)
    mine, grad_qr = lax.optimization_barrier((mine, grad_qr))
    parts = lax.all_to_all(
        mine, "head", 0, 0, tiled=True, axis_index_groups=[[0, 2, 4, 6], [1, 3, 5, 7]]
    ).reshape(4, tokens // 4, 640)
    share = tokens // 8
    kept, given = call(
        share_kernel, (parts,), [VMEM], [((share, 640), f32), ((share, 640), bf16)], [], 0.01
    )
    got = lax.ppermute(given, "head", [(h, h ^ 1) for h in range(8)])
    lat_grad, rope_grad = call(
        last_kernel, (kept, got), [VMEM] * 2, [((share, width), bf16), ((share, 64), bf16)], [], 0.01
    )
    return grad_q.reshape(tokens, heads, width), grad_qr, lat_grad, rope_grad


def solution(mesh):
    return jax.shard_map(
        shards,
        mesh=mesh,
        in_specs=(
            P("seq", "head", None),
            P("seq", "head"),
            P("seq", "head", None),
            P("seq", None),
            P(None, "seq"),
            P("head", "seq"),
            P("head", "seq"),
            P(),
        ),
        out_specs=(
            P("seq", "head", None),
            P("seq", "head"),
            P(("seq", "head"), None),
            P(("seq", "head"), None),
        ),
        check_vma=False,
    )
```

```python
import jax
import jax.numpy as jnp
from jax import lax
from jax.experimental import pallas as pl
from jax.experimental.pallas import tpu as pltpu
from jax.sharding import PartitionSpec as P

SPAN = 4
SOFTMAX_SCALE = 192.0 ** (-0.5)
BLK = 64
RUN = 16
WIDE = 640


def permute(value, to):
    seqs, heads = lax.axis_size("seq"), lax.axis_size("head")
    pairs = []
    for i in range(seqs):
        if to(i) is None:
            continue
        j = to(i) % seqs
        for h in range(heads):
            pairs.append((i * heads + h, j * heads + (h ^ 1 if i // RUN != j // RUN else h)))
    return lax.ppermute(value, ("seq", "head"), pairs)


def shift(value, by):
    return permute(value, lambda i: i + by)


def swap_cores(value):
    return permute(value, lambda i: i ^ 1)


def nt(a, b):
    return lax.dot_general(a, b, (((1,), (1,)), ((), ())), preferred_element_type=jnp.float32)


def nn(a, b):
    return lax.dot_general(a, b, (((1,), (0,)), ((), ())), preferred_element_type=jnp.float32)


def tn(a, b):
    return lax.dot_general(a, b, (((0,), (0,)), ((), ())), preferred_element_type=jnp.float32)


def rope_of(packed):
    wide = jnp.concatenate([packed[:, 128 * b : 128 * (b + 1)] for b in range(4)], axis=0)
    return wide.astype(jnp.float32).T.astype(jnp.bfloat16)


def gather_keys(order_ref, me, shards_in_order, refs, bases, rope_ref):
    seqs = order_ref.shape[0] // 2
    low, high = [], []
    for place, s in enumerate(shards_in_order):
        other = lax.rem(me + seqs - s, seqs)
        first, second = order_ref[2 * other], order_ref[2 * other + 1]
        low_slot = jnp.where(first < second, 0, 1)
        at_low = pl.multiple_of(low_slot * BLK, BLK)
        at_high = pl.multiple_of((1 - low_slot) * BLK, BLK)
        rope_ref[place] = rope_of(refs[place][pl.ds(bases[place] + 2 * BLK, 16), :])
        for out, at, pos in ((low, at_low, jnp.minimum(first, second)), (high, at_high, jnp.maximum(first, second))):
            out.append((refs[place][pl.ds(pl.multiple_of(bases[place] + at, 16), BLK), :], rope_ref[place, pl.ds(at, BLK), :], pos, at))
    both = low + high
    keys = jnp.concatenate([x[0] for x in both], axis=0)
    ropes = jnp.concatenate([x[1] for x in both], axis=0)
    return keys, ropes, [x[2] for x in both], [x[3] for x in both]


def own_place(order_ref, me, rows):
    first, second = order_ref[2 * me], order_ref[2 * me + 1]
    high = jnp.where(first > second, 0, 1)
    upper = pl.multiple_of(high * rows, rows)
    lower = pl.multiple_of((1 - high) * rows, rows)
    return jnp.minimum(first, second), jnp.maximum(first, second), lower, upper


def tile(keys, ropes, key_blocks, row_block, q, qr, do, total, dots):
    rows = q.shape[0]
    scores = SOFTMAX_SCALE * (nt(keys, q) + nt(ropes, qr))
    probs = jnp.exp(scores - total)
    ahead = (
        lax.broadcasted_iota(jnp.int32, (BLK, rows), 1) // (rows // BLK)
        - lax.broadcasted_iota(jnp.int32, (BLK, rows), 0)
    )
    pieces = []
    for n, key_block in enumerate(key_blocks):
        piece = probs[n * BLK : (n + 1) * BLK]
        if key_block is not None:
            piece = jnp.where(ahead >= (key_block - row_block) * BLK, piece, 0.0)
        pieces.append(piece)
    probs = jnp.concatenate(pieces, axis=0)
    dprobs = nt(keys, do)
    dscores = (SOFTMAX_SCALE * probs * (dprobs - dots)).astype(jnp.bfloat16)
    return probs.astype(jnp.bfloat16), dscores


def pack_kernel(lat_hbm, rope_hbm, order_hbm, dot_hbm, tot_hbm, own_ref, order_ref, dot_ref, tot_ref, sems):
    pairs = [(lat_hbm, own_ref.at[pl.ds(0, 128), :])]
    for b in range(4):
        pairs.append((rope_hbm.at[pl.ds(16 * b, 16), :], own_ref.at[pl.ds(128, 16), pl.ds(128 * b, 128)]))
    pairs += [(order_hbm, order_ref), (dot_hbm, dot_ref), (tot_hbm, tot_ref)]
    copies = [pltpu.make_async_copy(pair[0], pair[1], sems.at[n]) for n, pair in enumerate(pairs)]
    for copy in copies:
        copy.start()
    for copy in copies:
        copy.wait()


def spread(values):
    heads, tokens = values.shape
    rows = heads * tokens
    pieces, rest = [], values
    for _ in range(3):
        piece = rest.astype(jnp.bfloat16)
        rest = rest - piece.astype(jnp.float32)
        pieces.append(piece)
    column = lax.broadcasted_iota(jnp.int32, (tokens, rows), 1)
    token = lax.broadcasted_iota(jnp.int32, (tokens, rows), 0)
    pick = jnp.where(column // heads == token, 1.0, 0.0).astype(jnp.bfloat16)
    wide = (nn(pieces[0], pick) + nn(pieces[1], pick)) + nn(pieces[2], pick)
    column = lax.broadcasted_iota(jnp.int32, (heads, rows), 1)
    head = lax.broadcasted_iota(jnp.int32, (heads, rows), 0)
    return jnp.sum(jnp.where(lax.rem(column, heads) == head, wide, 0.0), axis=0, keepdims=True)


def window_part(order_ref, me, shards, refs, rope_ref, q_ref, qr_ref, do_ref, dot_ref, tot_ref, outs):
    ds_up_ref, ds_low_ref, keys_ref, ropes_ref = outs
    rows = q_ref.shape[0] // 2
    low_mine, high_mine, lower, upper = own_place(order_ref, me, rows)
    keys, ropes, blocks, at = gather_keys(order_ref, me, shards, refs, (0, 0), rope_ref)
    keys_ref[...] = keys
    ropes_ref[...] = ropes

    def grads(part, key_rows, row_block, seen, ds_ref):
        q, qr, do = q_ref[part, :], qr_ref[part, :], do_ref[part, :]
        probs, ds = tile(
            keys[:key_rows], ropes[:key_rows], seen, row_block, q, qr, do, tot_ref[:, part], dot_ref[:, part]
        )
        ds_ref[...] = ds
        return nn(ds, q) + nn(probs, do), nn(ds, qr)

    lat, grope = grads(pl.ds(upper, rows), 4 * BLK, high_mine, [None, None] + blocks[2:], ds_up_ref)
    lat_low, grope_low = grads(pl.ds(lower, rows), 2 * BLK, low_mine, blocks[:2], ds_low_ref)
    blank = jnp.zeros((BLK, WIDE - 512 - 64), jnp.float32)
    found = []
    for n in range(4):
        cut = slice(n * BLK, (n + 1) * BLK)
        lat_n, grope_n = lat[cut], grope[cut]
        if n < 2:
            lat_n, grope_n = lat_n + lat_low[cut], grope_n + grope_low[cut]
        found.append((at[n], jnp.concatenate([lat_n, grope_n, blank], axis=1)))
    return (found[0], found[2]), (found[1], found[3])


def early_kernel(
    order_ref, own_ref, near_ref, q_ref, qr_ref, do_ref, dot_in, tot_in,
    keep_ref, out_ref, ds_up_ref, ds_low_ref, keys_ref, ropes_ref, dot_ref, tot_ref,
    rope_ref,
):
    me = lax.axis_index("seq")
    dot_ref[...] = spread(dot_in[...])
    tot_ref[...] = spread(tot_in[...])
    shards = (0, jnp.where(lax.rem(me, 2) == 0, 3, 1))
    found = window_part(
        order_ref, me, shards, (own_ref, near_ref), rope_ref, q_ref, qr_ref, do_ref, dot_ref, tot_ref,
        (ds_up_ref, ds_low_ref, keys_ref, ropes_ref),
    )
    for at, value in found[0]:
        keep_ref[pl.ds(at, BLK), :] = value
    for at, value in found[1]:
        out_ref[pl.ds(at, BLK), :] = value.astype(jnp.bfloat16)


def late_kernel(
    order_ref, two_ref, last_ref, q_ref, qr_ref, do_ref, dot_ref, tot_ref,
    keep_ref, out_ref, ds_up_ref, ds_low_ref, keys_ref, ropes_ref,
    rope_ref,
):
    me = lax.axis_index("seq")
    shards = (2, jnp.where(lax.rem(me, 2) == 0, 1, 3))
    found = window_part(
        order_ref, me, shards, (two_ref, last_ref), rope_ref, q_ref, qr_ref, do_ref, dot_ref, tot_ref,
        (ds_up_ref, ds_low_ref, keys_ref, ropes_ref),
    )
    for at, value in found[0]:
        keep_ref[pl.ds(at, BLK), :] = value
    for at, value in found[1]:
        out_ref[pl.ds(at, BLK), :] = value.astype(jnp.bfloat16)


def query_kernel(
    order_ref, up_a_ref, low_a_ref, keys_a_ref, ropes_a_ref, up_b_ref, low_b_ref, keys_b_ref, ropes_b_ref,
    gq_ref, gqr_ref,
):
    me = lax.axis_index("seq")
    rows = up_a_ref.shape[1]
    _, _, lower, upper = own_place(order_ref, me, rows)
    half = 2 * BLK
    for at, a_ref, b_ref, n in ((upper, up_a_ref, up_b_ref, 2 * half), (lower, low_a_ref, low_b_ref, half)):
        part = pl.ds(at, rows)
        ds = jnp.concatenate([a_ref[...], b_ref[...]], axis=0)
        keys = jnp.concatenate([keys_a_ref[:n], keys_b_ref[:n]], axis=0)
        ropes = jnp.concatenate([ropes_a_ref[:n], ropes_b_ref[:n]], axis=0)
        gq_ref[part, :] = tn(ds, keys).astype(jnp.bfloat16)
        gqr_ref[part, :] = tn(ds, ropes).astype(jnp.bfloat16)


VMEM = pl.BlockSpec(memory_space=pltpu.VMEM)
SMEM = pl.BlockSpec(memory_space=pltpu.SMEM)
HBM = pl.BlockSpec(memory_space=pltpu.HBM)


def in_hbm(value):
    return pltpu.with_memory_space_constraint(value, pltpu.HBM)


def call(kernel, args, in_specs, outs, scratch, gflop, aliases={}):
    return pl.pallas_call(
        kernel,
        out_shape=tuple(jax.ShapeDtypeStruct(shape, dtype) for shape, dtype in outs),
        in_specs=in_specs,
        out_specs=(VMEM,) * len(outs),
        scratch_shapes=scratch,
        input_output_aliases=aliases,
        compiler_params=pltpu.CompilerParams(vmem_limit_bytes=32 * 2**20),
        cost_estimate=pl.CostEstimate(
            flops=int(gflop * 1e9), bytes_accessed=int(gflop * 2e6), transcendentals=int(gflop * 1e5)
        ),
    )(*args)


def first_join_kernel(keep_ref, two_ref, early_ref, home_ref, back_ref):
    even = lax.rem(lax.axis_index("seq"), 2) == 0
    early = early_ref[...].astype(jnp.float32)
    home_ref[...] = (keep_ref[...] + jnp.where(even, early, 0.0)).astype(jnp.bfloat16)
    back_ref[...] = two_ref[...] + jnp.where(even, 0.0, early)


def join_kernel(home_ref, back_ref, late_ref, out_ref):
    back = back_ref[...] + late_ref[...].astype(jnp.float32)
    rows = home_ref.shape[0] // 4
    for y in range(4):
        cut = slice(y * rows, (y + 1) * rows)
        out_ref[pl.ds(2 * y * rows, rows), :] = home_ref[cut]
        out_ref[pl.ds((2 * y + 1) * rows, rows), :] = back[cut].astype(jnp.bfloat16)


def y_kernel(parts_ref, keep_ref, send_ref):
    whole = parts_ref[0].astype(jnp.float32)
    for n in range(1, parts_ref.shape[0]):
        whole = whole + parts_ref[n].astype(jnp.float32)
    rows = keep_ref.shape[0]
    keep_ref[...] = whole[:rows]
    send_ref[...] = whole[rows:].astype(jnp.bfloat16)


def share_kernel(mine_ref, got_ref, keep_ref, send_ref):
    whole = mine_ref[...] + got_ref[...].astype(jnp.float32)
    rows = keep_ref.shape[0]
    first = lax.rem(lax.axis_index("head"), 2) == 0
    keep_ref[...] = jnp.where(first, whole[:rows], whole[rows:])
    send_ref[...] = jnp.where(first, whole[rows:], whole[:rows]).astype(jnp.bfloat16)


def last_kernel(keep_ref, got_ref, lat_ref, rope_ref):
    whole = keep_ref[...] + got_ref[...].astype(jnp.float32)
    lat_ref[...] = whole[:, :512].astype(jnp.bfloat16)
    rope_ref[...] = whole[:, 512:576].astype(jnp.bfloat16)


def shards(q_lat, q_rope, d_out, latent, key_rope, forward_dot, log_total, block_order):
    tokens, heads, width = q_lat.shape
    rows = tokens * heads
    half, bf16, f32 = rows // 2, jnp.bfloat16, jnp.float32
    own, order, dots, sums = call(
        pack_kernel,
        tuple(in_hbm(x) for x in (latent, key_rope, block_order, forward_dot, log_total)),
        [HBM] * 5,
        [
            ((tokens + 16, width), bf16),
            (block_order.shape, jnp.int32),
            (forward_dot.shape, f32),
            (log_total.shape, f32),
        ],
        [pltpu.SemaphoreType.DMA((8,))],
        20.0,
    )
    first = permute(own, lambda i: i + 3 if i % 2 else i + 1)
    two_back = shift(own, 2)
    last = permute(own, lambda i: i + 1 if i % 2 else i + 3)
    q, qr, do = q_lat.reshape(rows, width), q_rope.reshape(rows, 64), d_out.reshape(rows, width)
    kept = [((256, half), bf16), ((128, half), bf16), ((256, width), bf16), ((256, 64), bf16)]
    whole, vector = ((rows, width), bf16), ((1, rows), f32)
    keep, far, up_a, low_a, keys_a, ropes_a, dots, sums = call(
        early_kernel,
        (
            order, own, first, q, qr, do, dots, sums,
        ),
        [SMEM] + [VMEM] * 7,
        [((tokens, WIDE), f32), ((tokens, WIDE), bf16)] + kept + [vector, vector],
        [pltpu.VMEM((2, 128, 64), bf16)],
        0.0,
    )
    early_sent = shift(far, -1)
    two, other, up_b, low_b, keys_b, ropes_b = call(
        late_kernel,
        (order, two_back, last, q, qr, do, dots, sums),
        [SMEM] + [VMEM] * 7,
        [((tokens, WIDE), f32), ((tokens, WIDE), bf16)] + kept,
        [pltpu.VMEM((2, 128, 64), bf16)],
        0.0,
    )
    late_sent = swap_cores(other)
    grad_q, grad_qr = call(
        query_kernel,
        (order, up_a, low_a, keys_a, ropes_a, up_b, low_b, keys_b, ropes_b),
        [SMEM] + [VMEM] * 8,
        [whole, ((rows, 64), bf16)],
        [],
        0.05,
    )
    grad_qr = grad_qr.reshape(tokens, heads * 64)
    home, back = call(
        first_join_kernel,
        (keep, two, early_sent),
        [VMEM] * 3,
        [((tokens, WIDE), bf16), ((tokens, WIDE), f32)],
        [],
        0.0,
    )
    (joined,) = call(join_kernel, (home, back, late_sent), [VMEM] * 3, [((2 * tokens, WIDE), bf16)], [], 0.0)
    parts = lax.all_to_all(
        joined, "head", 0, 0, tiled=True, axis_index_groups=[[0, 2, 4, 6], [1, 3, 5, 7]]
    ).reshape(4, tokens // 2, WIDE)
    quarter, share = tokens // 4, tokens // 8
    mine, passed = call(
        y_kernel, (parts,), [VMEM], [((quarter, WIDE), f32), ((quarter, WIDE), bf16)], [], 0.0
    )
    kept, given = call(
        share_kernel,
        (mine, shift(passed, -2)),
        [VMEM] * 2,
        [((share, WIDE), f32), ((share, WIDE), bf16)],
        [],
        0.0,
    )
    got = lax.ppermute(given, "head", [(h, h ^ 1) for h in range(8)])
    lat_grad, rope_grad = call(
        last_kernel, (kept, got), [VMEM] * 2, [((share, width), bf16), ((share, 64), bf16)], [], 0.0
    )
    return grad_q.reshape(tokens, heads, width), grad_qr, lat_grad, rope_grad


def solution(mesh):
    return jax.shard_map(
        shards,
        mesh=mesh,
        in_specs=(
            P("seq", "head", None),
            P("seq", "head"),
            P("seq", "head", None),
            P("seq", None),
            P(None, "seq"),
            P("head", "seq"),
            P("head", "seq"),
            P(),
        ),
        out_specs=(
            P("seq", "head", None),
            P("seq", "head"),
            P(("seq", "head"), None),
            P(("seq", "head"), None),
        ),
        check_vma=False,
    )
```

```python
import jax
import jax.numpy as jnp
from jax import lax
from jax.experimental import pallas as pl
from jax.experimental.pallas import tpu as pltpu
from jax.sharding import PartitionSpec as P

SPAN = 4
SOFTMAX_SCALE = 192.0 ** (-0.5)
BLK = 64
RUN = 16
WIDE = 640


def permute(value, to):
    seqs, heads = lax.axis_size("seq"), lax.axis_size("head")
    pairs = []
    for i in range(seqs):
        if to(i) is None:
            continue
        j = to(i) % seqs
        for h in range(heads):
            pairs.append((i * heads + h, j * heads + (h ^ 1 if i // RUN != j // RUN else h)))
    return lax.ppermute(value, ("seq", "head"), pairs)


def shift(value, by):
    return permute(value, lambda i: i + by)


def swap_cores(value):
    return permute(value, lambda i: i ^ 1)


def nt(a, b):
    return lax.dot_general(a, b, (((1,), (1,)), ((), ())), preferred_element_type=jnp.float32)


def nn(a, b):
    return lax.dot_general(a, b, (((1,), (0,)), ((), ())), preferred_element_type=jnp.float32)


def tn(a, b):
    return lax.dot_general(a, b, (((0,), (0,)), ((), ())), preferred_element_type=jnp.float32)


def rope_of(packed):
    wide = jnp.concatenate([packed[:, 128 * b : 128 * (b + 1)] for b in range(4)], axis=0)
    return wide.astype(jnp.float32).T.astype(jnp.bfloat16)


def gather_keys(order_ref, me, shards_in_order, refs, bases, rope_ref):
    seqs = order_ref.shape[0] // 2
    low, high = [], []
    for place, s in enumerate(shards_in_order):
        other = lax.rem(me + seqs - s, seqs)
        first, second = order_ref[2 * other], order_ref[2 * other + 1]
        low_slot = jnp.where(first < second, 0, 1)
        at_low = pl.multiple_of(low_slot * BLK, BLK)
        at_high = pl.multiple_of((1 - low_slot) * BLK, BLK)
        rope_ref[place] = rope_of(refs[place][pl.ds(bases[place] + 2 * BLK, 16), :])
        for out, at, pos in ((low, at_low, jnp.minimum(first, second)), (high, at_high, jnp.maximum(first, second))):
            out.append((refs[place][pl.ds(pl.multiple_of(bases[place] + at, 16), BLK), :], rope_ref[place, pl.ds(at, BLK), :], pos, at))
    both = low + high
    keys = jnp.concatenate([x[0] for x in both], axis=0)
    ropes = jnp.concatenate([x[1] for x in both], axis=0)
    return keys, ropes, [x[2] for x in both], [x[3] for x in both]


def own_place(order_ref, me, rows):
    first, second = order_ref[2 * me], order_ref[2 * me + 1]
    high = jnp.where(first > second, 0, 1)
    upper = pl.multiple_of(high * rows, rows)
    lower = pl.multiple_of((1 - high) * rows, rows)
    return jnp.minimum(first, second), jnp.maximum(first, second), lower, upper


def tile(keys, ropes, key_blocks, row_block, q, qr, do, total, dots):
    rows = q.shape[0]
    scores = SOFTMAX_SCALE * (nt(keys, q) + nt(ropes, qr))
    probs = jnp.exp(scores - total)
    ahead = (
        lax.broadcasted_iota(jnp.int32, (BLK, rows), 1) // (rows // BLK)
        - lax.broadcasted_iota(jnp.int32, (BLK, rows), 0)
    )
    pieces = []
    for n, key_block in enumerate(key_blocks):
        piece = probs[n * BLK : (n + 1) * BLK]
        if key_block is not None:
            piece = jnp.where(ahead >= (key_block - row_block) * BLK, piece, 0.0)
        pieces.append(piece)
    probs = jnp.concatenate(pieces, axis=0)
    dprobs = nt(keys, do)
    dscores = (SOFTMAX_SCALE * probs * (dprobs - dots)).astype(jnp.bfloat16)
    return probs.astype(jnp.bfloat16), dscores


def pack_kernel(lat_hbm, rope_hbm, order_hbm, dot_hbm, tot_hbm, own_ref, order_ref, dot_ref, tot_ref, sems):
    pairs = [(lat_hbm, own_ref.at[pl.ds(0, 128), :])]
    for b in range(4):
        pairs.append((rope_hbm.at[pl.ds(16 * b, 16), :], own_ref.at[pl.ds(128, 16), pl.ds(128 * b, 128)]))
    pairs += [(order_hbm, order_ref), (dot_hbm, dot_ref), (tot_hbm, tot_ref)]
    copies = [pltpu.make_async_copy(pair[0], pair[1], sems.at[n]) for n, pair in enumerate(pairs)]
    for copy in copies:
        copy.start()
    for copy in copies:
        copy.wait()


def spread(values):
    heads, tokens = values.shape
    rows = heads * tokens
    pieces, rest = [], values
    for _ in range(3):
        piece = rest.astype(jnp.bfloat16)
        rest = rest - piece.astype(jnp.float32)
        pieces.append(piece)
    column = lax.broadcasted_iota(jnp.int32, (tokens, rows), 1)
    token = lax.broadcasted_iota(jnp.int32, (tokens, rows), 0)
    pick = jnp.where(column // heads == token, 1.0, 0.0).astype(jnp.bfloat16)
    wide = (nn(pieces[0], pick) + nn(pieces[1], pick)) + nn(pieces[2], pick)
    column = lax.broadcasted_iota(jnp.int32, (heads, rows), 1)
    head = lax.broadcasted_iota(jnp.int32, (heads, rows), 0)
    return jnp.sum(jnp.where(lax.rem(column, heads) == head, wide, 0.0), axis=0, keepdims=True)


def window_part(order_ref, me, shards, refs, rope_ref, q_ref, qr_ref, do_ref, dot_ref, tot_ref, outs):
    ds_up_ref, ds_low_ref, keys_ref, ropes_ref = outs
    rows = q_ref.shape[0] // 2
    low_mine, high_mine, lower, upper = own_place(order_ref, me, rows)
    keys, ropes, blocks, at = gather_keys(order_ref, me, shards, refs, (0, 0), rope_ref)
    keys_ref[...] = keys
    ropes_ref[...] = ropes

    def grads(part, key_rows, row_block, seen, ds_ref):
        q, qr, do = q_ref[part, :], qr_ref[part, :], do_ref[part, :]
        probs, ds = tile(
            keys[:key_rows], ropes[:key_rows], seen, row_block, q, qr, do, tot_ref[:, part], dot_ref[:, part]
        )
        ds_ref[...] = ds
        return nn(ds, q) + nn(probs, do), nn(ds, qr)

    lat, grope = grads(pl.ds(upper, rows), 4 * BLK, high_mine, [None, None] + blocks[2:], ds_up_ref)
    lat_low, grope_low = grads(pl.ds(lower, rows), 2 * BLK, low_mine, blocks[:2], ds_low_ref)
    blank = jnp.zeros((BLK, WIDE - 512 - 64), jnp.float32)
    found = []
    for n in range(4):
        cut = slice(n * BLK, (n + 1) * BLK)
        lat_n, grope_n = lat[cut], grope[cut]
        if n < 2:
            lat_n, grope_n = lat_n + lat_low[cut], grope_n + grope_low[cut]
        found.append((at[n], jnp.concatenate([lat_n, grope_n, blank], axis=1)))
    return (found[0], found[2]), (found[1], found[3])


def early_kernel(
    order_ref, own_ref, near_ref, q_ref, qr_ref, do_ref, dot_in, tot_in,
    keep_ref, out_ref, ds_up_ref, ds_low_ref, keys_ref, ropes_ref, dot_ref, tot_ref,
    rope_ref,
):
    me = lax.axis_index("seq")
    dot_ref[...] = spread(dot_in[...])
    tot_ref[...] = spread(tot_in[...])
    shards = (0, jnp.where(lax.rem(me, 2) == 0, 3, 1))
    found = window_part(
        order_ref, me, shards, (own_ref, near_ref), rope_ref, q_ref, qr_ref, do_ref, dot_ref, tot_ref,
        (ds_up_ref, ds_low_ref, keys_ref, ropes_ref),
    )
    for at, value in found[0]:
        keep_ref[pl.ds(at, BLK), :] = value
    for at, value in found[1]:
        out_ref[pl.ds(at, BLK), :] = value.astype(jnp.bfloat16)


def late_kernel(
    order_ref, two_ref, last_ref, q_ref, qr_ref, do_ref, dot_ref, tot_ref,
    keep_ref, out_ref, ds_up_ref, ds_low_ref, keys_ref, ropes_ref,
    rope_ref,
):
    me = lax.axis_index("seq")
    shards = (2, jnp.where(lax.rem(me, 2) == 0, 1, 3))
    found = window_part(
        order_ref, me, shards, (two_ref, last_ref), rope_ref, q_ref, qr_ref, do_ref, dot_ref, tot_ref,
        (ds_up_ref, ds_low_ref, keys_ref, ropes_ref),
    )
    for at, value in found[0]:
        keep_ref[pl.ds(at, BLK), :] = value
    for at, value in found[1]:
        out_ref[pl.ds(at, BLK), :] = value.astype(jnp.bfloat16)


def query_kernel(
    order_ref, up_a_ref, low_a_ref, keys_a_ref, ropes_a_ref, up_b_ref, low_b_ref, keys_b_ref, ropes_b_ref,
    gq_ref, gqr_ref,
):
    me = lax.axis_index("seq")
    rows = up_a_ref.shape[1]
    _, _, lower, upper = own_place(order_ref, me, rows)
    half = 2 * BLK
    for at, a_ref, b_ref, n in ((upper, up_a_ref, up_b_ref, 2 * half), (lower, low_a_ref, low_b_ref, half)):
        part = pl.ds(at, rows)
        ds = jnp.concatenate([a_ref[...], b_ref[...]], axis=0)
        keys = jnp.concatenate([keys_a_ref[:n], keys_b_ref[:n]], axis=0)
        ropes = jnp.concatenate([ropes_a_ref[:n], ropes_b_ref[:n]], axis=0)
        gq_ref[part, :] = tn(ds, keys).astype(jnp.bfloat16)
        gqr_ref[part, :] = tn(ds, ropes).astype(jnp.bfloat16)


VMEM = pl.BlockSpec(memory_space=pltpu.VMEM)
SMEM = pl.BlockSpec(memory_space=pltpu.SMEM)
HBM = pl.BlockSpec(memory_space=pltpu.HBM)


def in_hbm(value):
    return pltpu.with_memory_space_constraint(value, pltpu.HBM)


def call(kernel, args, in_specs, outs, scratch, gflop, aliases={}):
    return pl.pallas_call(
        kernel,
        out_shape=tuple(jax.ShapeDtypeStruct(shape, dtype) for shape, dtype in outs),
        in_specs=in_specs,
        out_specs=(VMEM,) * len(outs),
        scratch_shapes=scratch,
        input_output_aliases=aliases,
        compiler_params=pltpu.CompilerParams(vmem_limit_bytes=32 * 2**20),
        cost_estimate=pl.CostEstimate(
            flops=int(gflop * 1e9), bytes_accessed=int(gflop * 2e6), transcendentals=int(gflop * 1e5)
        ),
    )(*args)


def first_join_kernel(keep_ref, two_ref, early_ref, home_ref, back_ref):
    even = lax.rem(lax.axis_index("seq"), 2) == 0
    early = early_ref[...].astype(jnp.float32)
    home_ref[...] = (keep_ref[...] + jnp.where(even, early, 0.0)).astype(jnp.bfloat16)
    back_ref[...] = two_ref[...] + jnp.where(even, 0.0, early)


def join_kernel(home_ref, back_ref, late_ref, out_ref):
    back = back_ref[...] + late_ref[...].astype(jnp.float32)
    out_ref[:, :512] = home_ref[:, :512]
    out_ref[:, 512:1024] = back[:, :512].astype(jnp.bfloat16)
    ropes = jnp.concatenate([home_ref[:, 512:576].astype(jnp.float32), back[:, 512:576]], axis=1)
    out_ref[:, 1024:] = ropes.astype(jnp.bfloat16)


def y_kernel(parts_ref, keep_ref, send_ref):
    whole = parts_ref[0].astype(jnp.float32)
    for n in range(1, parts_ref.shape[0]):
        whole = whole + parts_ref[n].astype(jnp.float32)
    ropes = whole[:, 1024:]
    keep_ref[:, :512] = whole[:, :512]
    keep_ref[:, 512:] = ropes
    send_ref[:, :512] = whole[:, 512:1024].astype(jnp.bfloat16)
    send_ref[:, 512:] = jnp.concatenate([ropes[:, 64:], ropes[:, :64]], axis=1).astype(jnp.bfloat16)


def share_kernel(mine_ref, got_ref, keep_ref, send_ref):
    whole = mine_ref[...] + got_ref[...].astype(jnp.float32)
    rows = keep_ref.shape[0]
    first = lax.rem(lax.axis_index("head"), 2) == 0
    keep_ref[...] = jnp.where(first, whole[:rows], whole[rows:])
    send_ref[...] = jnp.where(first, whole[rows:], whole[:rows]).astype(jnp.bfloat16)


def last_kernel(keep_ref, got_ref, lat_ref, rope_ref):
    whole = keep_ref[...] + got_ref[...].astype(jnp.float32)
    lat_ref[...] = whole[:, :512].astype(jnp.bfloat16)
    rope_ref[...] = whole[:, 512:576].astype(jnp.bfloat16)


def shards(q_lat, q_rope, d_out, latent, key_rope, forward_dot, log_total, block_order):
    tokens, heads, width = q_lat.shape
    rows = tokens * heads
    half, bf16, f32 = rows // 2, jnp.bfloat16, jnp.float32
    own, order, dots, sums = call(
        pack_kernel,
        tuple(in_hbm(x) for x in (latent, key_rope, block_order, forward_dot, log_total)),
        [HBM] * 5,
        [
            ((tokens + 16, width), bf16),
            (block_order.shape, jnp.int32),
            (forward_dot.shape, f32),
            (log_total.shape, f32),
        ],
        [pltpu.SemaphoreType.DMA((8,))],
        20.0,
    )
    first = permute(own, lambda i: i + 3 if i % 2 else i + 1)
    two_back = shift(own, 2)
    last = permute(own, lambda i: i + 1 if i % 2 else i + 3)
    q, qr, do = q_lat.reshape(rows, width), q_rope.reshape(rows, 64), d_out.reshape(rows, width)
    kept = [((256, half), bf16), ((128, half), bf16), ((256, width), bf16), ((256, 64), bf16)]
    whole, vector = ((rows, width), bf16), ((1, rows), f32)
    keep, far, up_a, low_a, keys_a, ropes_a, dots, sums = call(
        early_kernel,
        (
            order, own, first, q, qr, do, dots, sums,
        ),
        [SMEM] + [VMEM] * 7,
        [((tokens, WIDE), f32), ((tokens, WIDE), bf16)] + kept + [vector, vector],
        [pltpu.VMEM((2, 128, 64), bf16)],
        0.0,
    )
    early_sent = shift(far, -1)
    two, other, up_b, low_b, keys_b, ropes_b = call(
        late_kernel,
        (order, two_back, last, q, qr, do, dots, sums),
        [SMEM] + [VMEM] * 7,
        [((tokens, WIDE), f32), ((tokens, WIDE), bf16)] + kept,
        [pltpu.VMEM((2, 128, 64), bf16)],
        0.0,
    )
    late_sent = swap_cores(other)
    grad_q, grad_qr = call(
        query_kernel,
        (order, up_a, low_a, keys_a, ropes_a, up_b, low_b, keys_b, ropes_b),
        [SMEM] + [VMEM] * 8,
        [whole, ((rows, 64), bf16)],
        [],
        0.05,
    )
    grad_qr = grad_qr.reshape(tokens, heads * 64)
    home, back = call(
        first_join_kernel,
        (keep, two, early_sent),
        [VMEM] * 3,
        [((tokens, WIDE), bf16), ((tokens, WIDE), f32)],
        [],
        0.0,
    )
    (joined,) = call(join_kernel, (home, back, late_sent), [VMEM] * 3, [((tokens, 1152), bf16)], [], 0.0)
    parts = lax.all_to_all(
        joined, "head", 0, 0, tiled=True, axis_index_groups=[[0, 2, 4, 6], [1, 3, 5, 7]]
    ).reshape(4, tokens // 4, 1152)
    quarter, share = tokens // 4, tokens // 8
    mine, passed = call(
        y_kernel, (parts,), [VMEM], [((quarter, WIDE), f32), ((quarter, WIDE), bf16)], [], 0.0
    )
    kept, given = call(
        share_kernel,
        (mine, shift(passed, -2)),
        [VMEM] * 2,
        [((share, WIDE), f32), ((share, WIDE), bf16)],
        [],
        0.0,
    )
    got = lax.ppermute(given, "head", [(h, h ^ 1) for h in range(8)])
    lat_grad, rope_grad = call(
        last_kernel, (kept, got), [VMEM] * 2, [((share, width), bf16), ((share, 64), bf16)], [], 0.0
    )
    return grad_q.reshape(tokens, heads, width), grad_qr, lat_grad, rope_grad


def solution(mesh):
    return jax.shard_map(
        shards,
        mesh=mesh,
        in_specs=(
            P("seq", "head", None),
            P("seq", "head"),
            P("seq", "head", None),
            P("seq", None),
            P(None, "seq"),
            P("head", "seq"),
            P("head", "seq"),
            P(),
        ),
        out_specs=(
            P("seq", "head", None),
            P("seq", "head"),
            P(("seq", "head"), None),
            P(("seq", "head"), None),
        ),
        check_vma=False,
    )
```

```python
import jax
import jax.numpy as jnp
from jax import lax
from jax.experimental import pallas as pl
from jax.experimental.pallas import tpu as pltpu
from jax.sharding import PartitionSpec as P

SPAN = 4
SOFTMAX_SCALE = 192.0 ** (-0.5)
BLK = 64
RUN = 16
WIDE = 640


def permute(value, to):
    seqs, heads = lax.axis_size("seq"), lax.axis_size("head")
    pairs = []
    for i in range(seqs):
        if to(i) is None:
            continue
        j = to(i) % seqs
        for h in range(heads):
            pairs.append((i * heads + h, j * heads + (h ^ 1 if i // RUN != j // RUN else h)))
    return lax.ppermute(value, ("seq", "head"), pairs)


def shift(value, by):
    return permute(value, lambda i: i + by)


def swap_cores(value):
    return permute(value, lambda i: i ^ 1)


def nt(a, b):
    return lax.dot_general(a, b, (((1,), (1,)), ((), ())), preferred_element_type=jnp.float32)


def nn(a, b):
    return lax.dot_general(a, b, (((1,), (0,)), ((), ())), preferred_element_type=jnp.float32)


def tn(a, b):
    return lax.dot_general(a, b, (((0,), (0,)), ((), ())), preferred_element_type=jnp.float32)


def rope_of(packed):
    wide = jnp.concatenate([packed[:, 128 * b : 128 * (b + 1)] for b in range(4)], axis=0)
    return wide.astype(jnp.float32).T.astype(jnp.bfloat16)


def gather_keys(order_ref, me, shards_in_order, refs, bases, rope_ref):
    seqs = order_ref.shape[0] // 2
    low, high = [], []
    for place, s in enumerate(shards_in_order):
        other = lax.rem(me + seqs - s, seqs)
        first, second = order_ref[2 * other], order_ref[2 * other + 1]
        low_slot = jnp.where(first < second, 0, 1)
        at_low = pl.multiple_of(low_slot * BLK, BLK)
        at_high = pl.multiple_of((1 - low_slot) * BLK, BLK)
        rope_ref[place] = rope_of(refs[place][pl.ds(bases[place] + 2 * BLK, 16), :])
        for out, at, pos in ((low, at_low, jnp.minimum(first, second)), (high, at_high, jnp.maximum(first, second))):
            out.append((refs[place][pl.ds(pl.multiple_of(bases[place] + at, 16), BLK), :], rope_ref[place, pl.ds(at, BLK), :], pos, at))
    both = low + high
    keys = jnp.concatenate([x[0] for x in both], axis=0)
    ropes = jnp.concatenate([x[1] for x in both], axis=0)
    return keys, ropes, [x[2] for x in both], [x[3] for x in both]


def own_place(order_ref, me, rows):
    first, second = order_ref[2 * me], order_ref[2 * me + 1]
    high = jnp.where(first > second, 0, 1)
    upper = pl.multiple_of(high * rows, rows)
    lower = pl.multiple_of((1 - high) * rows, rows)
    return jnp.minimum(first, second), jnp.maximum(first, second), lower, upper


def products(keys, ropes, q, qr, do):
    return nt(keys, q) + nt(ropes, qr), nt(keys, do)


def weigh(scores, dprobs, key_blocks, row_block, total, dots):
    rows = scores.shape[1]
    probs = jnp.exp(SOFTMAX_SCALE * scores - total)
    ahead = (
        lax.broadcasted_iota(jnp.int32, (BLK, rows), 1) // (rows // BLK)
        - lax.broadcasted_iota(jnp.int32, (BLK, rows), 0)
    )
    pieces = []
    for n, key_block in enumerate(key_blocks):
        piece = probs[n * BLK : (n + 1) * BLK]
        if key_block is not None:
            piece = jnp.where(ahead >= (key_block - row_block) * BLK, piece, 0.0)
        pieces.append(piece)
    probs = jnp.concatenate(pieces, axis=0)
    dscores = (SOFTMAX_SCALE * probs * (dprobs - dots)).astype(jnp.bfloat16)
    return probs.astype(jnp.bfloat16), dscores


def pack_kernel(
    lat_hbm, rope_hbm, order_hbm, dot_hbm, tot_hbm, own_ref, order_ref, dot_ref, tot_ref, rope_ref, sems
):
    pairs = (
        (rope_hbm, rope_ref),
        (lat_hbm, own_ref.at[pl.ds(0, 128), :]),
        (dot_hbm, dot_ref),
        (tot_hbm, tot_ref),
        (order_hbm, order_ref),
    )
    copies = [pltpu.make_async_copy(pair[0], pair[1], sems.at[n]) for n, pair in enumerate(pairs)]
    for copy in copies:
        copy.start()
    copies[0].wait()
    for b in range(4):
        own_ref[128:, 128 * b : 128 * (b + 1)] = rope_ref[16 * b : 16 * (b + 1), :]
    for copy in copies[1:]:
        copy.wait()


def spread(values):
    heads, tokens = values.shape
    rows = heads * tokens
    pieces, rest = [], values
    for _ in range(3):
        piece = rest.astype(jnp.bfloat16)
        rest = rest - piece.astype(jnp.float32)
        pieces.append(piece)
    column = lax.broadcasted_iota(jnp.int32, (tokens, rows), 1)
    token = lax.broadcasted_iota(jnp.int32, (tokens, rows), 0)
    pick = jnp.where(column // heads == token, 1.0, 0.0).astype(jnp.bfloat16)
    wide = (nn(pieces[0], pick) + nn(pieces[1], pick)) + nn(pieces[2], pick)
    column = lax.broadcasted_iota(jnp.int32, (heads, rows), 1)
    head = lax.broadcasted_iota(jnp.int32, (heads, rows), 0)
    return jnp.sum(jnp.where(lax.rem(column, heads) == head, wide, 0.0), axis=0, keepdims=True)


def window_part(order_ref, me, shards, refs, rope_ref, q_ref, qr_ref, do_ref, dot_ref, tot_ref, outs):
    ds_up_ref, ds_low_ref, keys_ref, ropes_ref = outs
    rows = q_ref.shape[0] // 2
    low_mine, high_mine, lower, upper = own_place(order_ref, me, rows)
    keys, ropes, blocks, at = gather_keys(order_ref, me, shards, refs, (0, 0), rope_ref)
    keys_ref[...] = keys
    ropes_ref[...] = ropes

    up, low = pl.ds(upper, rows), pl.ds(lower, rows)
    s_up, d_up = products(keys, ropes, q_ref[up, :], qr_ref[up, :], do_ref[up, :])
    s_low, d_low = products(keys[: 2 * BLK], ropes[: 2 * BLK], q_ref[low, :], qr_ref[low, :], do_ref[low, :])
    p_up, ds_up = weigh(s_up, d_up, [None, None] + blocks[2:], high_mine, tot_ref[:, up], dot_ref[:, up])
    ds_up_ref[...] = ds_up
    p_low, ds_low = weigh(s_low, d_low, blocks[:2], low_mine, tot_ref[:, low], dot_ref[:, low])
    ds_low_ref[...] = ds_low
    lat = nn(ds_up, q_ref[up, :]) + nn(p_up, do_ref[up, :])
    grope = nn(ds_up, qr_ref[up, :])
    lat_low = nn(ds_low, q_ref[low, :]) + nn(p_low, do_ref[low, :])
    grope_low = nn(ds_low, qr_ref[low, :])
    blank = jnp.zeros((BLK, WIDE - 512 - 64), jnp.float32)
    found = []
    for n in range(4):
        cut = slice(n * BLK, (n + 1) * BLK)
        lat_n, grope_n = lat[cut], grope[cut]
        if n < 2:
            lat_n, grope_n = lat_n + lat_low[cut], grope_n + grope_low[cut]
        found.append((at[n], jnp.concatenate([lat_n, grope_n, blank], axis=1)))
    return (found[0], found[2]), (found[1], found[3])


def early_kernel(
    order_ref, own_ref, near_ref, q_ref, qr_ref, do_ref, dot_in, tot_in,
    keep_ref, out_ref, ds_up_ref, ds_low_ref, keys_ref, ropes_ref, dot_ref, tot_ref,
    rope_ref,
):
    me = lax.axis_index("seq")
    dot_ref[...] = spread(dot_in[...])
    tot_ref[...] = spread(tot_in[...])
    shards = (0, jnp.where(lax.rem(me, 2) == 0, 3, 1))
    found = window_part(
        order_ref, me, shards, (own_ref, near_ref), rope_ref, q_ref, qr_ref, do_ref, dot_ref, tot_ref,
        (ds_up_ref, ds_low_ref, keys_ref, ropes_ref),
    )
    for at, value in found[0]:
        keep_ref[pl.ds(at, BLK), :] = value
    for at, value in found[1]:
        out_ref[pl.ds(at, BLK), :] = value.astype(jnp.bfloat16)


def late_kernel(
    order_ref, two_ref, last_ref, q_ref, qr_ref, do_ref, dot_ref, tot_ref,
    keep_ref, out_ref, ds_up_ref, ds_low_ref, keys_ref, ropes_ref,
    rope_ref,
):
    me = lax.axis_index("seq")
    shards = (2, jnp.where(lax.rem(me, 2) == 0, 1, 3))
    found = window_part(
        order_ref, me, shards, (two_ref, last_ref), rope_ref, q_ref, qr_ref, do_ref, dot_ref, tot_ref,
        (ds_up_ref, ds_low_ref, keys_ref, ropes_ref),
    )
    for at, value in found[0]:
        keep_ref[pl.ds(at, BLK), :] = value
    for at, value in found[1]:
        out_ref[pl.ds(at, BLK), :] = value.astype(jnp.bfloat16)


def query_kernel(
    order_ref, up_a_ref, low_a_ref, keys_a_ref, ropes_a_ref, up_b_ref, low_b_ref, keys_b_ref, ropes_b_ref,
    gq_ref, gqr_ref,
):
    me = lax.axis_index("seq")
    rows = up_a_ref.shape[1]
    _, _, lower, upper = own_place(order_ref, me, rows)
    half = 2 * BLK
    for at, a_ref, b_ref, n in ((upper, up_a_ref, up_b_ref, 2 * half), (lower, low_a_ref, low_b_ref, half)):
        part = pl.ds(at, rows)
        ds = jnp.concatenate([a_ref[...], b_ref[...]], axis=0)
        keys = jnp.concatenate([keys_a_ref[:n], keys_b_ref[:n]], axis=0)
        ropes = jnp.concatenate([ropes_a_ref[:n], ropes_b_ref[:n]], axis=0)
        gq_ref[part, :] = tn(ds, keys).astype(jnp.bfloat16)
        gqr_ref[part, :] = tn(ds, ropes).astype(jnp.bfloat16)


VMEM = pl.BlockSpec(memory_space=pltpu.VMEM)
SMEM = pl.BlockSpec(memory_space=pltpu.SMEM)
HBM = pl.BlockSpec(memory_space=pltpu.HBM)


def in_hbm(value):
    return pltpu.with_memory_space_constraint(value, pltpu.HBM)


def call(kernel, args, in_specs, outs, scratch, gflop, aliases={}):
    return pl.pallas_call(
        kernel,
        out_shape=tuple(jax.ShapeDtypeStruct(shape, dtype) for shape, dtype in outs),
        in_specs=in_specs,
        out_specs=(VMEM,) * len(outs),
        scratch_shapes=scratch,
        input_output_aliases=aliases,
        compiler_params=pltpu.CompilerParams(vmem_limit_bytes=32 * 2**20),
        cost_estimate=pl.CostEstimate(
            flops=int(gflop * 1e9), bytes_accessed=int(gflop * 2e6), transcendentals=int(gflop * 1e5)
        ),
    )(*args)


def first_join_kernel(keep_ref, two_ref, early_ref, home_ref, back_ref):
    even = lax.rem(lax.axis_index("seq"), 2) == 0
    early = early_ref[...].astype(jnp.float32)
    home_ref[...] = (keep_ref[...] + jnp.where(even, early, 0.0)).astype(jnp.bfloat16)
    back_ref[...] = two_ref[...] + jnp.where(even, 0.0, early)


def join_kernel(home_ref, back_ref, late_ref, out_ref):
    back = back_ref[...] + late_ref[...].astype(jnp.float32)
    out_ref[:, :512] = home_ref[:, :512]
    out_ref[:, 512:1024] = back[:, :512].astype(jnp.bfloat16)
    ropes = jnp.concatenate([home_ref[:, 512:576].astype(jnp.float32), back[:, 512:576]], axis=1)
    out_ref[:, 1024:] = ropes.astype(jnp.bfloat16)


def y_kernel(parts_ref, keep_ref, send_ref):
    whole = parts_ref[0].astype(jnp.float32)
    for n in range(1, parts_ref.shape[0]):
        whole = whole + parts_ref[n].astype(jnp.float32)
    ropes = whole[:, 1024:]
    keep_ref[:, :512] = whole[:, :512]
    keep_ref[:, 512:] = ropes
    send_ref[:, :512] = whole[:, 512:1024].astype(jnp.bfloat16)
    send_ref[:, 512:] = jnp.concatenate([ropes[:, 64:], ropes[:, :64]], axis=1).astype(jnp.bfloat16)


def share_kernel(mine_ref, got_ref, keep_ref, send_ref):
    whole = mine_ref[...] + got_ref[...].astype(jnp.float32)
    rows = keep_ref.shape[0]
    first = lax.rem(lax.axis_index("head"), 2) == 0
    keep_ref[...] = jnp.where(first, whole[:rows], whole[rows:])
    send_ref[...] = jnp.where(first, whole[rows:], whole[:rows]).astype(jnp.bfloat16)


def last_kernel(keep_ref, got_ref, lat_ref, rope_ref):
    whole = keep_ref[...] + got_ref[...].astype(jnp.float32)
    lat_ref[...] = whole[:, :512].astype(jnp.bfloat16)
    rope_ref[...] = whole[:, 512:576].astype(jnp.bfloat16)


def shards(q_lat, q_rope, d_out, latent, key_rope, forward_dot, log_total, block_order):
    tokens, heads, width = q_lat.shape
    rows = tokens * heads
    half, bf16, f32 = rows // 2, jnp.bfloat16, jnp.float32
    own, order, dots, sums = call(
        pack_kernel,
        tuple(in_hbm(x) for x in (latent, key_rope, block_order, forward_dot, log_total)),
        [HBM] * 5,
        [
            ((tokens + 16, width), bf16),
            (block_order.shape, jnp.int32),
            (forward_dot.shape, f32),
            (log_total.shape, f32),
        ],
        [pltpu.VMEM((64, 128), bf16), pltpu.SemaphoreType.DMA((5,))],
        20.0,
    )
    first = permute(own, lambda i: i + 3 if i % 2 else i + 1)
    two_back = shift(own, 2)
    last = permute(own, lambda i: i + 1 if i % 2 else i + 3)
    q, qr, do = q_lat.reshape(rows, width), q_rope.reshape(rows, 64), d_out.reshape(rows, width)
    kept = [((256, half), bf16), ((128, half), bf16), ((256, width), bf16), ((256, 64), bf16)]
    whole, vector = ((rows, width), bf16), ((1, rows), f32)
    keep, far, up_a, low_a, keys_a, ropes_a, dots, sums = call(
        early_kernel,
        (
            order, own, first, q, qr, do, dots, sums,
        ),
        [SMEM] + [VMEM] * 7,
        [((tokens, WIDE), f32), ((tokens, WIDE), bf16)] + kept + [vector, vector],
        [pltpu.VMEM((2, 128, 64), bf16)],
        0.0,
    )
    early_sent = shift(far, -1)
    two, other, up_b, low_b, keys_b, ropes_b = call(
        late_kernel,
        (order, two_back, last, q, qr, do, dots, sums),
        [SMEM] + [VMEM] * 7,
        [((tokens, WIDE), f32), ((tokens, WIDE), bf16)] + kept,
        [pltpu.VMEM((2, 128, 64), bf16)],
        0.0,
    )
    late_sent = swap_cores(other)
    grad_q, grad_qr = call(
        query_kernel,
        (order, up_a, low_a, keys_a, ropes_a, up_b, low_b, keys_b, ropes_b),
        [SMEM] + [VMEM] * 8,
        [whole, ((rows, 64), bf16)],
        [],
        0.05,
    )
    grad_qr = grad_qr.reshape(tokens, heads * 64)
    home, back = call(
        first_join_kernel,
        (keep, two, early_sent),
        [VMEM] * 3,
        [((tokens, WIDE), bf16), ((tokens, WIDE), f32)],
        [],
        0.0,
    )
    (joined,) = call(join_kernel, (home, back, late_sent), [VMEM] * 3, [((tokens, 1152), bf16)], [], 0.0)
    parts = lax.all_to_all(
        joined, "head", 0, 0, tiled=True, axis_index_groups=[[0, 2, 4, 6], [1, 3, 5, 7]]
    ).reshape(4, tokens // 4, 1152)
    quarter, share = tokens // 4, tokens // 8
    mine, passed = call(
        y_kernel, (parts,), [VMEM], [((quarter, WIDE), f32), ((quarter, WIDE), bf16)], [], 0.0
    )
    kept, given = call(
        share_kernel,
        (mine, shift(passed, -2)),
        [VMEM] * 2,
        [((share, WIDE), f32), ((share, WIDE), bf16)],
        [],
        0.0,
    )
    got = lax.ppermute(given, "head", [(h, h ^ 1) for h in range(8)])
    lat_grad, rope_grad = call(
        last_kernel, (kept, got), [VMEM] * 2, [((share, width), bf16), ((share, 64), bf16)], [], 0.0
    )
    return grad_q.reshape(tokens, heads, width), grad_qr, lat_grad, rope_grad


def solution(mesh):
    return jax.shard_map(
        shards,
        mesh=mesh,
        in_specs=(
            P("seq", "head", None),
            P("seq", "head"),
            P("seq", "head", None),
            P("seq", None),
            P(None, "seq"),
            P("head", "seq"),
            P("head", "seq"),
            P(),
        ),
        out_specs=(
            P("seq", "head", None),
            P("seq", "head"),
            P(("seq", "head"), None),
            P(("seq", "head"), None),
        ),
        check_vma=False,
    )
```

```python
import jax
import jax.numpy as jnp
from jax import lax
from jax.experimental import pallas as pl
from jax.experimental.pallas import tpu as pltpu
from jax.sharding import PartitionSpec as P

SPAN = 4
SOFTMAX_SCALE = 192.0 ** (-0.5)
BLK = 64
RUN = 16
WIDE = 640


def permute(value, to):
    seqs, heads = lax.axis_size("seq"), lax.axis_size("head")
    pairs = []
    for i in range(seqs):
        if to(i) is None:
            continue
        j = to(i) % seqs
        for h in range(heads):
            pairs.append((i * heads + h, j * heads + (h ^ 1 if i // RUN != j // RUN else h)))
    return lax.ppermute(value, ("seq", "head"), pairs)


def shift(value, by):
    return permute(value, lambda i: i + by)


def swap_cores(value):
    return permute(value, lambda i: i ^ 1)


def nt(a, b):
    return lax.dot_general(a, b, (((1,), (1,)), ((), ())), preferred_element_type=jnp.float32)


def nn(a, b):
    return lax.dot_general(a, b, (((1,), (0,)), ((), ())), preferred_element_type=jnp.float32)


def tn(a, b):
    return lax.dot_general(a, b, (((0,), (0,)), ((), ())), preferred_element_type=jnp.float32)


def rope_of(packed):
    wide = jnp.concatenate([packed[:, 128 * b : 128 * (b + 1)] for b in range(4)], axis=0)
    return wide.astype(jnp.float32).T.astype(jnp.bfloat16)


def gather_keys(order_ref, me, shards_in_order, refs, bases, rope_ref):
    seqs = order_ref.shape[0] // 2
    low, high = [], []
    for place, s in enumerate(shards_in_order):
        other = lax.rem(me + seqs - s, seqs)
        first, second = order_ref[2 * other], order_ref[2 * other + 1]
        low_slot = jnp.where(first < second, 0, 1)
        at_low = pl.multiple_of(low_slot * BLK, BLK)
        at_high = pl.multiple_of((1 - low_slot) * BLK, BLK)
        rope_ref[place] = rope_of(refs[place][pl.ds(bases[place] + 2 * BLK, 16), :])
        for out, at, pos in ((low, at_low, jnp.minimum(first, second)), (high, at_high, jnp.maximum(first, second))):
            out.append((refs[place][pl.ds(pl.multiple_of(bases[place] + at, 16), BLK), :], rope_ref[place, pl.ds(at, BLK), :], pos, at))
    both = low + high
    keys = jnp.concatenate([x[0] for x in both], axis=0)
    ropes = jnp.concatenate([x[1] for x in both], axis=0)
    return keys, ropes, [x[2] for x in both], [x[3] for x in both]


def own_place(order_ref, me, rows):
    first, second = order_ref[2 * me], order_ref[2 * me + 1]
    high = jnp.where(first > second, 0, 1)
    upper = pl.multiple_of(high * rows, rows)
    lower = pl.multiple_of((1 - high) * rows, rows)
    return jnp.minimum(first, second), jnp.maximum(first, second), lower, upper


def tile(keys, ropes, key_blocks, row_block, q, qr, do, total, dots):
    rows = q.shape[0]
    scores = nt(keys, q) + nt(ropes, qr)
    probs = jnp.exp(SOFTMAX_SCALE * scores - total)
    ahead = (
        lax.broadcasted_iota(jnp.int32, (BLK, rows), 1) // (rows // BLK)
        - lax.broadcasted_iota(jnp.int32, (BLK, rows), 0)
    )
    pieces = []
    for n, key_block in enumerate(key_blocks):
        piece = probs[n * BLK : (n + 1) * BLK]
        if key_block is not None:
            piece = jnp.where(ahead >= (key_block - row_block) * BLK, piece, 0.0)
        pieces.append(piece)
    probs = jnp.concatenate(pieces, axis=0)
    dprobs = nt(keys, do)
    dscores = (probs * (SOFTMAX_SCALE * dprobs - dots)).astype(jnp.bfloat16)
    return probs.astype(jnp.bfloat16), dscores


def pack_kernel(lat_hbm, rope_hbm, order_hbm, dot_hbm, tot_hbm, own_ref, order_ref, dot_ref, tot_ref, sems):
    pairs = [(lat_hbm, own_ref.at[pl.ds(0, 128), :])]
    for b in range(4):
        pairs.append((rope_hbm.at[pl.ds(16 * b, 16), :], own_ref.at[pl.ds(128, 16), pl.ds(128 * b, 128)]))
    pairs += [(order_hbm, order_ref), (dot_hbm, dot_ref), (tot_hbm, tot_ref)]
    copies = [pltpu.make_async_copy(pair[0], pair[1], sems.at[n]) for n, pair in enumerate(pairs)]
    for copy in copies:
        copy.start()
    for copy in copies:
        copy.wait()


def spread(values):
    heads, tokens = values.shape
    rows = heads * tokens
    pieces, rest = [], values
    for _ in range(3):
        piece = rest.astype(jnp.bfloat16)
        rest = rest - piece.astype(jnp.float32)
        pieces.append(piece)
    column = lax.broadcasted_iota(jnp.int32, (tokens, rows), 1)
    token = lax.broadcasted_iota(jnp.int32, (tokens, rows), 0)
    pick = jnp.where(column // heads == token, 1.0, 0.0).astype(jnp.bfloat16)
    wide = (nn(pieces[0], pick) + nn(pieces[1], pick)) + nn(pieces[2], pick)
    column = lax.broadcasted_iota(jnp.int32, (heads, rows), 1)
    head = lax.broadcasted_iota(jnp.int32, (heads, rows), 0)
    return jnp.sum(jnp.where(lax.rem(column, heads) == head, wide, 0.0), axis=0, keepdims=True)


def window_part(order_ref, me, shards, refs, rope_ref, q_ref, qr_ref, do_ref, dot_ref, tot_ref, outs):
    ds_up_ref, ds_low_ref, keys_ref, ropes_ref = outs
    rows = q_ref.shape[0] // 2
    low_mine, high_mine, lower, upper = own_place(order_ref, me, rows)
    keys, ropes, blocks, at = gather_keys(order_ref, me, shards, refs, (0, 0), rope_ref)
    keys_ref[...] = keys
    ropes_ref[...] = ropes

    def grads(part, key_rows, row_block, seen, ds_ref):
        q, qr, do = q_ref[part, :], qr_ref[part, :], do_ref[part, :]
        probs, ds = tile(
            keys[:key_rows], ropes[:key_rows], seen, row_block, q, qr, do, tot_ref[:, part], dot_ref[:, part]
        )
        ds_ref[...] = ds
        return nn(ds, q) + nn(probs, do), nn(ds, qr)

    lat, grope = grads(pl.ds(upper, rows), 4 * BLK, high_mine, [None, None] + blocks[2:], ds_up_ref)
    lat_low, grope_low = grads(pl.ds(lower, rows), 2 * BLK, low_mine, blocks[:2], ds_low_ref)
    blank = jnp.zeros((BLK, WIDE - 512 - 64), jnp.float32)
    found = []
    for n in range(4):
        cut = slice(n * BLK, (n + 1) * BLK)
        lat_n, grope_n = lat[cut], grope[cut]
        if n < 2:
            lat_n, grope_n = lat_n + lat_low[cut], grope_n + grope_low[cut]
        found.append((at[n], jnp.concatenate([lat_n, grope_n, blank], axis=1)))
    return (found[0], found[2]), (found[1], found[3])


def early_kernel(
    order_ref, own_ref, near_ref, q_ref, qr_ref, do_ref, dot_in, tot_in,
    keep_ref, out_ref, ds_up_ref, ds_low_ref, keys_ref, ropes_ref, dot_ref, tot_ref,
    rope_ref,
):
    me = lax.axis_index("seq")
    dot_ref[...] = SOFTMAX_SCALE * spread(dot_in[...])
    tot_ref[...] = spread(tot_in[...])
    shards = (0, jnp.where(lax.rem(me, 2) == 0, 3, 1))
    found = window_part(
        order_ref, me, shards, (own_ref, near_ref), rope_ref, q_ref, qr_ref, do_ref, dot_ref, tot_ref,
        (ds_up_ref, ds_low_ref, keys_ref, ropes_ref),
    )
    for at, value in found[0]:
        keep_ref[pl.ds(at, BLK), :] = value
    for at, value in found[1]:
        out_ref[pl.ds(at, BLK), :] = value.astype(jnp.bfloat16)


def late_kernel(
    order_ref, two_ref, last_ref, q_ref, qr_ref, do_ref, dot_ref, tot_ref,
    keep_ref, out_ref, ds_up_ref, ds_low_ref, keys_ref, ropes_ref,
    rope_ref,
):
    me = lax.axis_index("seq")
    shards = (2, jnp.where(lax.rem(me, 2) == 0, 1, 3))
    found = window_part(
        order_ref, me, shards, (two_ref, last_ref), rope_ref, q_ref, qr_ref, do_ref, dot_ref, tot_ref,
        (ds_up_ref, ds_low_ref, keys_ref, ropes_ref),
    )
    for at, value in found[0]:
        keep_ref[pl.ds(at, BLK), :] = value
    for at, value in found[1]:
        out_ref[pl.ds(at, BLK), :] = value.astype(jnp.bfloat16)


def query_kernel(
    order_ref, up_a_ref, low_a_ref, keys_a_ref, ropes_a_ref, up_b_ref, low_b_ref, keys_b_ref, ropes_b_ref,
    gq_ref, gqr_ref,
):
    me = lax.axis_index("seq")
    rows = up_a_ref.shape[1]
    _, _, lower, upper = own_place(order_ref, me, rows)
    half = 2 * BLK
    for at, a_ref, b_ref, n in ((upper, up_a_ref, up_b_ref, 2 * half), (lower, low_a_ref, low_b_ref, half)):
        part = pl.ds(at, rows)
        ds = jnp.concatenate([a_ref[...], b_ref[...]], axis=0)
        keys = jnp.concatenate([keys_a_ref[:n], keys_b_ref[:n]], axis=0)
        ropes = jnp.concatenate([ropes_a_ref[:n], ropes_b_ref[:n]], axis=0)
        gq_ref[part, :] = tn(ds, keys).astype(jnp.bfloat16)
        gqr_ref[part, :] = tn(ds, ropes).astype(jnp.bfloat16)


VMEM = pl.BlockSpec(memory_space=pltpu.VMEM)
SMEM = pl.BlockSpec(memory_space=pltpu.SMEM)
HBM = pl.BlockSpec(memory_space=pltpu.HBM)


def in_hbm(value):
    return pltpu.with_memory_space_constraint(value, pltpu.HBM)


def call(kernel, args, in_specs, outs, scratch, gflop, aliases={}):
    return pl.pallas_call(
        kernel,
        out_shape=tuple(jax.ShapeDtypeStruct(shape, dtype) for shape, dtype in outs),
        in_specs=in_specs,
        out_specs=(VMEM,) * len(outs),
        scratch_shapes=scratch,
        input_output_aliases=aliases,
        compiler_params=pltpu.CompilerParams(vmem_limit_bytes=32 * 2**20),
        cost_estimate=pl.CostEstimate(
            flops=int(gflop * 1e9), bytes_accessed=int(gflop * 2e6), transcendentals=int(gflop * 1e5)
        ),
    )(*args)


def first_join_kernel(keep_ref, two_ref, early_ref, home_ref, back_ref):
    even = lax.rem(lax.axis_index("seq"), 2) == 0
    early = early_ref[...].astype(jnp.float32)
    home_ref[...] = (keep_ref[...] + jnp.where(even, early, 0.0)).astype(jnp.bfloat16)
    back_ref[...] = two_ref[...] + jnp.where(even, 0.0, early)


def join_kernel(home_ref, back_ref, late_ref, out_ref):
    back = back_ref[...] + late_ref[...].astype(jnp.float32)
    out_ref[:, :512] = home_ref[:, :512]
    out_ref[:, 512:1024] = back[:, :512].astype(jnp.bfloat16)
    ropes = jnp.concatenate([home_ref[:, 512:576].astype(jnp.float32), back[:, 512:576]], axis=1)
    out_ref[:, 1024:] = ropes.astype(jnp.bfloat16)


def y_kernel(parts_ref, keep_ref, send_ref):
    whole = parts_ref[0].astype(jnp.float32)
    for n in range(1, parts_ref.shape[0]):
        whole = whole + parts_ref[n].astype(jnp.float32)
    ropes = whole[:, 1024:]
    keep_ref[:, :512] = whole[:, :512]
    keep_ref[:, 512:] = ropes
    send_ref[:, :512] = whole[:, 512:1024].astype(jnp.bfloat16)
    send_ref[:, 512:] = jnp.concatenate([ropes[:, 64:], ropes[:, :64]], axis=1).astype(jnp.bfloat16)


def share_kernel(mine_ref, got_ref, keep_ref, send_ref):
    whole = mine_ref[...] + got_ref[...].astype(jnp.float32)
    rows = keep_ref.shape[0]
    first = lax.rem(lax.axis_index("head"), 2) == 0
    keep_ref[...] = jnp.where(first, whole[:rows], whole[rows:])
    send_ref[...] = jnp.where(first, whole[rows:], whole[:rows]).astype(jnp.bfloat16)


def last_kernel(keep_ref, got_ref, lat_ref, rope_ref):
    whole = keep_ref[...] + got_ref[...].astype(jnp.float32)
    lat_ref[...] = whole[:, :512].astype(jnp.bfloat16)
    rope_ref[...] = whole[:, 512:576].astype(jnp.bfloat16)


def shards(q_lat, q_rope, d_out, latent, key_rope, forward_dot, log_total, block_order):
    tokens, heads, width = q_lat.shape
    rows = tokens * heads
    half, bf16, f32 = rows // 2, jnp.bfloat16, jnp.float32
    own, order, dots, sums = call(
        pack_kernel,
        tuple(in_hbm(x) for x in (latent, key_rope, block_order, forward_dot, log_total)),
        [HBM] * 5,
        [
            ((tokens + 16, width), bf16),
            (block_order.shape, jnp.int32),
            (forward_dot.shape, f32),
            (log_total.shape, f32),
        ],
        [pltpu.SemaphoreType.DMA((8,))],
        20.0,
    )
    first = permute(own, lambda i: i + 3 if i % 2 else i + 1)
    two_back = shift(own, 2)
    last = permute(own, lambda i: i + 1 if i % 2 else i + 3)
    q, qr, do = q_lat.reshape(rows, width), q_rope.reshape(rows, 64), d_out.reshape(rows, width)
    kept = [((256, half), bf16), ((128, half), bf16), ((256, width), bf16), ((256, 64), bf16)]
    whole, vector = ((rows, width), bf16), ((1, rows), f32)
    keep, far, up_a, low_a, keys_a, ropes_a, dots, sums = call(
        early_kernel,
        (
            order, own, first, q, qr, do, dots, sums,
        ),
        [SMEM] + [VMEM] * 7,
        [((tokens, WIDE), f32), ((tokens, WIDE), bf16)] + kept + [vector, vector],
        [pltpu.VMEM((2, 128, 64), bf16)],
        0.0,
    )
    early_sent = shift(far, -1)
    two, other, up_b, low_b, keys_b, ropes_b = call(
        late_kernel,
        (order, two_back, last, q, qr, do, dots, sums),
        [SMEM] + [VMEM] * 7,
        [((tokens, WIDE), f32), ((tokens, WIDE), bf16)] + kept,
        [pltpu.VMEM((2, 128, 64), bf16)],
        0.0,
    )
    late_sent = swap_cores(other)
    grad_q, grad_qr = call(
        query_kernel,
        (order, up_a, low_a, keys_a, ropes_a, up_b, low_b, keys_b, ropes_b),
        [SMEM] + [VMEM] * 8,
        [whole, ((rows, 64), bf16)],
        [],
        0.05,
    )
    grad_qr = grad_qr.reshape(tokens, heads * 64)
    home, back = call(
        first_join_kernel,
        (keep, two, early_sent),
        [VMEM] * 3,
        [((tokens, WIDE), bf16), ((tokens, WIDE), f32)],
        [],
        0.0,
    )
    (joined,) = call(join_kernel, (home, back, late_sent), [VMEM] * 3, [((tokens, 1152), bf16)], [], 0.0)
    parts = lax.all_to_all(
        joined, "head", 0, 0, tiled=True, axis_index_groups=[[0, 2, 4, 6], [1, 3, 5, 7]]
    ).reshape(4, tokens // 4, 1152)
    quarter, share = tokens // 4, tokens // 8
    mine, passed = call(
        y_kernel, (parts,), [VMEM], [((quarter, WIDE), f32), ((quarter, WIDE), bf16)], [], 0.0
    )
    kept, given = call(
        share_kernel,
        (mine, shift(passed, -2)),
        [VMEM] * 2,
        [((share, WIDE), f32), ((share, WIDE), bf16)],
        [],
        0.0,
    )
    got = lax.ppermute(given, "head", [(h, h ^ 1) for h in range(8)])
    lat_grad, rope_grad = call(
        last_kernel, (kept, got), [VMEM] * 2, [((share, width), bf16), ((share, 64), bf16)], [], 0.0
    )
    return grad_q.reshape(tokens, heads, width), grad_qr, lat_grad, rope_grad


def solution(mesh):
    return jax.shard_map(
        shards,
        mesh=mesh,
        in_specs=(
            P("seq", "head", None),
            P("seq", "head"),
            P("seq", "head", None),
            P("seq", None),
            P(None, "seq"),
            P("head", "seq"),
            P("head", "seq"),
            P(),
        ),
        out_specs=(
            P("seq", "head", None),
            P("seq", "head"),
            P(("seq", "head"), None),
            P(("seq", "head"), None),
        ),
        check_vma=False,
    )
```
